128 devices in a mesh: grp: 2 (over x_hi), slab: 64 (over y, z, x_lo, core).
Axes of the slice: x: 4 (x_hi: 2, x_lo: 2; x = x_hi * 2 + x_lo), y: 4, z: 4, core: 2. Of those that a mesh axis runs over, the one named last changes fastest.
Arguments:
- patterns: bfloat16 [2, 16384, 16384], P('grp', 'slab'), may hold values from 0.099609375 to 10
- probabilities: bfloat16 [2, 16384, 32], P('grp', 'slab'), may hold values from 1.9431114e-05 to 0.001953125
- source_row: int32 [2, 64, 64, 80], P('grp', 'slab'), may hold values from -1 to 4095, as said below
- target_row: int32 [2, 64, 64, 80], P('grp', 'slab'), may hold values from 0 to 2047
- support: int32 [256, 256, 256], P('slab', 'grp'), may hold values 0 or 1
- density: float32 [256, 256, 256], P('slab', 'grp'), may hold values from -6 to 6
Outputs:
- intensity: float32 [256, 256, 256], P('slab', 'grp')
- phased_density: float32 [256, 256, 256], P('slab', 'grp')
The draws below stay inside these ranges and needn't reach their ends.
Inputs may be any that keep to these rules, and one draw needn't show every extreme that they name: `source_row`: each device's table holds every one of its slice rows 0 to 4095 exactly once; -1 marks an empty slot; one slab owner, drawn from the seed, has all 80 slots filled from every device. target_row[g, o, s, c] is the half-row of owner o's slab for slot c of source_row[g, s, o]; it is arbitrary where that slot is -1.
All inputs are finite; a program needn't handle non-finite values. No bound on the sum of `support` on one device may be relied on, other than what follows from the above.
Results may differ from the reference program's by a relative error of at most 0.0015.
Values may be sent and summed in bfloat16 or wider, within the bound.
No kernel may reach another device: no remote copies, remote signals or barrier semaphores. Data moves between devices by JAX's collectives and lax.ppermute only.
A program may use at most 128 MiB of HBM per device.

```python
import math
import jax
import jax.numpy as jnp
from jax import lax

DET = 128
NV = 256
K_DEV = 256
R_BLK = 32
ITERS = 2
CAP = 80
PLANES = 4
PATTERNS = 16384
N_GRP = 2
N_SLAB = 64


def draw_source_row(key, part):
    key = jax.random.fold_in(key, 7)
    rows_total = R_BLK * DET
    spare = (N_SLAB - 1) * CAP
    fullest = jax.random.randint(jax.random.fold_in(key, 1), (), 0, N_SLAB)

    def one_device(device_key):
        first_key, second_key = jax.random.split(device_key)
        order = jax.random.permutation(first_key, spare)
        used = jnp.zeros((spare,), jnp.int32).at[order[:rows_total - CAP]].set(1)
        grid = jnp.concatenate([used.reshape(N_SLAB - 1, CAP), jnp.ones((1, CAP), jnp.int32)], axis=0)
        owners = (jnp.arange(N_SLAB, dtype=jnp.int32) - fullest - 1) % N_SLAB
        grid = grid[owners].reshape(-1)
        position = jnp.cumsum(grid) - 1
        shuffled = jax.random.permutation(second_key, rows_total).astype(jnp.int32)
        picked = shuffled[jnp.clip(position, 0, rows_total - 1)]
        return jnp.where(grid == 1, picked, -1).astype(jnp.int32).reshape(N_SLAB, CAP)
    device_keys = jax.random.split(jax.random.fold_in(key, 2), N_GRP * N_SLAB)
    return jax.vmap(one_device)(device_keys).reshape(N_GRP, N_SLAB, N_SLAB, CAP)


def touch_ends(array, stream_key, smallest, high):
    spot = [jax.random.randint(jax.random.fold_in(stream_key, axis), (), 0, length) for axis, length in enumerate(array.shape)]
    main_axis = array.shape.index(max(array.shape))
    next_to = spot[:main_axis] + [(spot[main_axis] + 1) % array.shape[main_axis]] + spot[main_axis + 1:]
    return array.at[tuple(spot)].set(smallest).at[tuple(next_to)].set(high)


def level_of(rng, extent, shards, least, top_value):
    factor_of = 1.0
    for dim, parts in shards:
        draws = jax.random.uniform(jax.random.fold_in(jax.random.fold_in(rng, 6), dim), (parts,), jnp.float32, least / len(shards), top_value / len(shards))
        factor_of = factor_of * jnp.repeat(jnp.exp(draws), extent[dim] // parts).reshape((-1,) + (1,) * (len(extent) - 1 - dim))
    return factor_of


def normal_values(rng, dims, scale, limit, cuts=(), kind=jnp.bfloat16):
    values = scale * jax.random.normal(rng, dims, jnp.float32)
    if cuts:
        values = values * level_of(rng, dims, cuts, -0.22, 0.18)
    return jnp.clip(values, -limit, limit).astype(kind)


def setup_inputs(seed: int = 0) -> dict:
    keys = jax.random.split(jax.random.key(seed), 7)
    patterns = jnp.clip(jnp.exp(math.log(10.0) - 4.609084 * jax.random.uniform(keys[0], (N_GRP, PATTERNS, DET * DET), jnp.float32) ** level_of(keys[0], (N_GRP, PATTERNS, DET * DET), ((0, 2), (1, 64)), -0.2, 0.2)), 0.099609375, 10.0).astype(jnp.bfloat16)
    probabilities = jnp.clip(jnp.exp(math.log(0.001953125) - 4.61031033 * jax.random.uniform(keys[1], (N_GRP, PATTERNS, R_BLK), jnp.float32) ** level_of(keys[1], (N_GRP, PATTERNS, R_BLK), ((0, 2), (1, 64)), -0.2, 0.2)), 1.9431114196777344e-05, 0.001953125).astype(jnp.bfloat16)
    source_row = draw_source_row(jax.random.fold_in(keys[6], 71), 0)
    target_row = touch_ends(jax.random.randint(keys[3], (N_GRP, N_SLAB, N_SLAB, CAP), 0, 2 * PLANES * NV), jax.random.fold_in(keys[3], 1), 0, (2 * PLANES * NV) - 1).astype(jnp.int32)
    support = touch_ends((jax.random.randint(keys[4], (NV, NV, NV), 0, 2) < 1).astype(jnp.int32), jax.random.fold_in(keys[4], 1), 0, 1)
    density = normal_values(keys[5], (NV, NV, NV), 1.0, 6.0, ((0, 64), (1, 2)), jnp.float32)
    return {"patterns": patterns, "probabilities": probabilities, "source_row": source_row, "target_row": target_row, "support": support, "density": density}


BETA = 0.9
SOFTEN = 0.25

def reference(patterns, probabilities, source_row, target_row, support, density):
    devices = N_GRP * N_SLAB
    half_rows = 2 * PLANES * NV
    pattern_blocks = patterns.reshape(devices, K_DEV, DET * DET)
    prob_blocks = probabilities.reshape(devices, K_DEV, R_BLK)
    sources = source_row.reshape(devices, N_SLAB * CAP)
    targets = jnp.swapaxes(target_row, 1, 2).reshape(devices, N_SLAB, CAP)
    offsets = (jnp.arange(N_SLAB, dtype=jnp.int32) * half_rows)[:, None]

    def merge(carry, inputs):
        summed, weights = carry
        block_pats, block_probs, source, target = inputs
        slices = jnp.dot(block_probs.T, block_pats, preferred_element_type=jnp.float32)
        rows = slices.astype(jnp.bfloat16).reshape(R_BLK * DET, DET)
        weight = lax.optimization_barrier(jnp.sum(block_probs.astype(jnp.float32), axis=0)).astype(jnp.bfloat16)
        valid = source >= 0
        safe = jnp.maximum(source, 0)
        values = jnp.where(valid[:, None], rows[safe].astype(jnp.float32), jnp.float32(0.0))
        row_weight = jnp.where(valid, weight[safe // DET].astype(jnp.float32), jnp.float32(0.0))
        place = (offsets + target).reshape(-1).astype(jnp.int32)
        return ((summed.at[place].add(values), weights.at[place].add(row_weight)), None)
    start = (jnp.zeros((NV * NV * 2, DET), jnp.float32), jnp.zeros((NV * NV * 2,), jnp.float32))
    (summed, weights), unused = lax.scan(merge, start, (pattern_blocks, prob_blocks, sources, targets))
    divisor = jnp.maximum(weights, 1.0).reshape(NV, NV, 2, 1)
    intensity = (summed.reshape(NV, NV, 2, DET) / divisor).reshape(NV, NV, NV)
    amplitude = jnp.sqrt(intensity)
    inside = support == 1
    field = density
    for step in range(ITERS):
        spectrum = jnp.fft.fftn(field, norm='ortho')
        scale = amplitude / jnp.sqrt(spectrum.real ** 2 + spectrum.imag ** 2 + SOFTEN)
        image = jnp.real(jnp.fft.ifftn(spectrum * scale, norm='ortho'))
        field = jnp.where(inside, image, field - BETA * image)
    return (intensity, field)
```

```python
import functools

import jax
import jax.numpy as jnp
import ml_dtypes
import numpy as np
from jax import lax
from jax.experimental import pallas as pl
from jax.experimental.pallas import tpu as pltpu
from jax.sharding import PartitionSpec as P

N = 256
HALF = N // 2
PLANES = 4
SLABS = 64
DEVS = 128
CAP = 80
ROWS = 4096
BETA = 0.9
SOFTEN = 0.25
BOTH = ("grp", "slab")
VMEM = 48 * 1024 * 1024


def split_table(table):
    high = table.astype(np.float32).astype(ml_dtypes.bfloat16)
    low = (table - high.astype(np.float64)).astype(np.float32).astype(ml_dtypes.bfloat16)
    return (jnp.asarray(high), jnp.asarray(low))


def phase(rows, columns):
    angle = 2.0 * np.pi / N * ((rows[:, None] * columns[None, :]) % N)
    return (np.cos(angle) / np.sqrt(N), np.sin(angle) / np.sqrt(N))


def complex_table(cos, sin):
    return np.block([[cos, -sin], [sin, cos]])


@functools.cache
def tables():
    z = np.arange(N)
    kz = np.arange(HALF)
    cos, sin = phase(z, kz)
    nyquist = np.cos(np.pi * z) / np.sqrt(N)
    forward_z = np.concatenate([cos, -sin], axis=1)
    forward_z[:, HALF] = nyquist
    inverse_z = np.concatenate([2.0 * cos.T, -2.0 * sin.T], axis=0)
    inverse_z[0] = 1.0 / np.sqrt(N)
    inverse_z[HALF] = nyquist
    y = np.arange(HALF)
    first = np.arange(DEVS)
    second = np.where(first == 0, HALF, N - first)
    cos_a, sin_a = phase(first, y)
    cos_b, sin_b = phase(second, y)
    forward_y = np.block([[cos_a, sin_a], [-sin_a, cos_a], [cos_b, sin_b], [-sin_b, cos_b]])
    inverse_y = np.block([[cos_a.T, -sin_a.T, cos_b.T, -sin_b.T], [sin_a.T, cos_a.T, sin_b.T, cos_b.T]])
    order = (np.arange(PLANES)[:, None] + PLANES * np.arange(SLABS)[None, :]).reshape(-1)
    cos, sin = phase(order, order)
    forward_x = complex_table(cos, -sin)
    cos_m, sin_m = phase(-order, order)
    mirror_x = complex_table(cos_m, -sin_m)
    inverse_x = complex_table(cos, sin)
    place = np.argsort(order)
    flip_x = np.zeros((N, N))
    flip_x[np.arange(N), place[(-order) % N]] = 1.0
    flip_z = np.zeros((N, N))
    flip_z[(-z) % N, z] = 1.0
    flip_y = np.zeros((2, HALF, HALF))
    flip_y[0] = np.eye(HALF)
    flip_y[1][y, (-y) % HALF] = 1.0
    return dict(
        forward_z=split_table(forward_z),
        inverse_z=split_table(inverse_z),
        forward_y=split_table(forward_y),
        inverse_y=split_table(inverse_y),
        forward_x=split_table(np.concatenate([forward_x, mirror_x], axis=0)),
        inverse_x=split_table(inverse_x),
        flip_x=jnp.asarray(flip_x.astype(ml_dtypes.bfloat16)),
        flip_z=jnp.asarray(flip_z.astype(ml_dtypes.bfloat16)),
        flip_y=jnp.asarray(flip_y.astype(ml_dtypes.bfloat16)),
    )


def halves(values):
    high = values.astype(jnp.bfloat16)
    return (high, (values - high.astype(jnp.float32)).astype(jnp.bfloat16))


def dot(left, right):
    return jnp.dot(left, right, preferred_element_type=jnp.float32)


def table_times(high, low, values):
    a, b = halves(values)
    return dot(high, a) + (dot(high, b) + dot(low, a))


def times_table(values, high, low):
    a, b = halves(values)
    return dot(a, high) + (dot(b, high) + dot(a, low))


def call(kernel, out_shape, **kwargs):
    return pl.pallas_call(
        kernel,
        out_shape=out_shape,
        compiler_params=pltpu.CompilerParams(vmem_limit_bytes=VMEM),
        **kwargs,
    )


def spec_vmem(count):
    return [pl.BlockSpec(memory_space=pltpu.VMEM)] * count


def smem():
    return pl.BlockSpec(memory_space=pltpu.SMEM)


OWNERS = 8
SLOTS = OWNERS * CAP
SEND = 88
DEEP = 1024


def gather_kernel(weight_ref, column_ref, table_ref, rows_ref, out_ref):
    source = column_ref[...]
    low = source & (DEEP - 1)
    high = source >> 10
    onehot = (low == lax.broadcasted_iota(jnp.int32, (SLOTS, DEEP), 1)).astype(jnp.bfloat16)
    rows = jnp.concatenate([rows_ref[q * DEEP : (q + 1) * DEEP] for q in range(4)], axis=1)
    wide = dot(onehot, rows)
    picked = jnp.where(high == 0, wide[:, :128], 0.0)
    for q in range(1, 4):
        picked = jnp.where(high == q, wide[:, q * 128 : (q + 1) * 128], picked)
    orientation = table_ref[...] >> 7
    weights = jnp.zeros((OWNERS, 128), jnp.float32)
    for r in range(32):
        weights = jnp.where(orientation == r, weight_ref[r], weights)
    top = lax.broadcasted_iota(jnp.int32, (8, 128), 0) == 0
    for o in range(OWNERS):
        last = jnp.where(top, weights[o : o + 1], 0.0)
        both = jnp.concatenate([picked[o * CAP : (o + 1) * CAP], last], axis=0)
        out_ref[o] = both.astype(jnp.bfloat16)


def gather_rows(weight, column, table, rows):
    return call(
        gather_kernel,
        jax.ShapeDtypeStruct((SLABS, SEND, 128), jnp.bfloat16),
        grid=(SLABS // OWNERS,),
        in_specs=[
            smem(),
            pl.BlockSpec((SLOTS, 1), lambda i: (i, 0)),
            pl.BlockSpec((OWNERS, 128), lambda i: (i, 0)),
            pl.BlockSpec((ROWS, 128), lambda i: (0, 0)),
        ],
        out_specs=pl.BlockSpec((OWNERS, SEND, 128), lambda i: (i, 0, 0)),
    )(weight, column, table, rows)


PAY = 24


def place_kernel(got_ref, column_ref, row_ref, out_ref, sum_ref, weight_ref):
    step = pl.program_id(0)

    @pl.when(step == 0)
    def start():
        sum_ref[...] = jnp.zeros_like(sum_ref)
        weight_ref[...] = jnp.zeros_like(weight_ref)

    column = column_ref[...]
    row = row_ref[0]
    rows = jnp.concatenate([got_ref[s, :CAP] for s in range(OWNERS)], axis=0)
    onehot = (lax.broadcasted_iota(jnp.int32, (512, SLOTS), 0) == (row & 511)).astype(jnp.bfloat16)
    quarter = column >> 9
    wide = jnp.concatenate([jnp.where(quarter == q, rows, jnp.bfloat16(0)) for q in range(4)], axis=1)
    sum_ref[...] += dot(onehot, wide)
    last = jnp.concatenate([got_ref[s, CAP:SEND].astype(jnp.float32)[:1] for s in range(OWNERS)], axis=0)
    turned = jnp.concatenate([last, jnp.zeros((120, 128), jnp.float32)], axis=0).T
    weights = jnp.concatenate([turned[:CAP, s : s + 1] for s in range(OWNERS)], axis=0)
    lane = lax.broadcasted_iota(jnp.int32, (SLOTS, 128), 1)
    right = jnp.where(lane == (column & 15), weights, 0.0).astype(jnp.bfloat16)
    left = (lax.broadcasted_iota(jnp.int32, (DEVS, SLOTS), 0) == (row >> 4)).astype(jnp.bfloat16)
    weight_ref[...] += dot(left, right)

    @pl.when(step == pl.num_programs(0) - 1)
    def end():
        for q in range(4):
            out_ref[q * 32 : (q + 1) * 32, :16, :] = sum_ref[:, q * 128 : (q + 1) * 128].reshape(32, 16, 128)
        out_ref[:, 16:, :] = jnp.broadcast_to(weight_ref[...][:, None, :], (DEVS, 8, 128))


def place_rows(got, column, row):
    return call(
        place_kernel,
        jax.ShapeDtypeStruct((DEVS, PAY, 128), jnp.float32),
        grid=(SLABS // OWNERS,),
        in_specs=[
            pl.BlockSpec((OWNERS, SEND, 128), lambda i: (i, 0, 0)),
            pl.BlockSpec((SLOTS, 1), lambda i: (i, 0)),
            pl.BlockSpec((1, 1, SLOTS), lambda i: (i, 0, 0)),
        ],
        out_specs=pl.BlockSpec((DEVS, PAY, 128), lambda i: (0, 0, 0)),
        scratch_shapes=[pltpu.VMEM((512, 512), jnp.float32), pltpu.VMEM((DEVS, 128), jnp.float32)],
    )(got, column, row)


def intensity_kernel(group_ref, own_ref, other_ref, flip_ref, out_ref):
    group = group_ref[0]
    weights = own_ref[:, 16, :] + other_ref[:, 8, :]
    divisor = jnp.maximum(jnp.where(group == 0, weights[:, :8], weights[:, 8:16]), 1.0)
    parts = []
    for q in range(8):
        total = jnp.where(group == 0, own_ref[:, q, :], own_ref[:, 8 + q, :]) + other_ref[:, q, :]
        parts.append(total / divisor[:, q : q + 1])
    wide = jnp.concatenate(parts, axis=1)
    flip = jnp.where(group == 0, flip_ref[0], flip_ref[1])
    high = wide.astype(jnp.bfloat16)
    rest = wide - high.astype(jnp.float32)
    middle = rest.astype(jnp.bfloat16)
    least = (rest - middle.astype(jnp.float32)).astype(jnp.bfloat16)
    turned = dot(flip, high) + (dot(flip, middle) + dot(flip, least))
    for x in range(PLANES):
        out_ref[x] = turned[:, x * N : (x + 1) * N]


def intensity_of(group, own, other, flip):
    return call(
        intensity_kernel,
        jax.ShapeDtypeStruct((PLANES, HALF, N), jnp.float32),
        in_specs=[smem()] + spec_vmem(3),
        out_specs=pl.BlockSpec(memory_space=pltpu.VMEM),
    )(group, own, other, flip)


def amplitude_kernel(first_ref, got_ref, flip_x_ref, flip_z_ref, out_ref, nyquist_ref):
    first = first_ref[0]
    divisor = jnp.maximum(got_ref[:SLABS, 16, :] + got_ref[SLABS:, 16, :], 1.0)
    amplitude = []
    for pm in range(2):
        columns = []
        for zh in range(2):
            planes = []
            for x in range(PLANES):
                q = (pm * PLANES + x) * 2 + zh
                total = got_ref[:SLABS, q, :] + got_ref[SLABS:, q, :]
                planes.append(jnp.sqrt(total / divisor[:, q : q + 1]))
            columns.append(jnp.concatenate(planes, axis=0))
        amplitude.append(jnp.concatenate(columns, axis=1))
    flip_x = flip_x_ref[...]
    flip_z = flip_z_ref[...]
    mirrored = []
    for pm in range(2):
        high, low = halves(amplitude[pm])
        high = dot(flip_x, high).astype(jnp.bfloat16)
        low = dot(flip_x, low).astype(jnp.bfloat16)
        mirrored.append(dot(high, flip_z) + dot(low, flip_z))
    for pm in range(2):
        partner = jnp.where(first == 1, mirrored[pm], mirrored[1 - pm])
        even = 0.5 * (amplitude[pm] + partner)
        out_ref[:, pm * HALF : (pm + 1) * HALF] = even[:, :HALF]
        nyquist_ref[:, pm * HALF : (pm + 1) * HALF] = even[:, HALF:]


def amplitude_of(first, got, flip_x, flip_z):
    return call(
        amplitude_kernel,
        (jax.ShapeDtypeStruct((N, N), jnp.float32),) * 2,
        in_specs=[smem()] + spec_vmem(3),
        out_specs=tuple(spec_vmem(2)),
    )(first, got, flip_x, flip_z)


def send_forward(field, forward_z, forward_y, out_ref):
    partly = times_table(field, forward_z[0][...], forward_z[1][...])
    columns = []
    for x in range(PLANES):
        block = partly[x * HALF : (x + 1) * HALF]
        columns.append(jnp.concatenate([block[:, :HALF], block[:, HALF:]], axis=0))
    result = table_times(forward_y[0][...], forward_y[1][...], jnp.concatenate(columns, axis=1))
    for x in range(PLANES):
        for q in range(4):
            out_ref[:, x * 4 + q, :] = result[q * DEVS : (q + 1) * DEVS, x * HALF : (x + 1) * HALF]


def image_from(got_ref, inverse_y, inverse_z):
    columns = []
    for x in range(PLANES):
        columns.append(jnp.concatenate([got_ref[:, x * 4 + q, :] for q in range(4)], axis=0))
    partly = table_times(inverse_y[0][...], inverse_y[1][...], jnp.concatenate(columns, axis=1))
    rows = []
    for x in range(PLANES):
        block = partly[:, x * HALF : (x + 1) * HALF]
        rows.append(jnp.concatenate([block[:HALF], block[HALF:]], axis=1))
    return times_table(jnp.concatenate(rows, axis=0), inverse_z[0][...], inverse_z[1][...])


def updated(image, support_ref, density_ref):
    support = support_ref[...].reshape(PLANES * HALF, N)
    density = density_ref[...].reshape(PLANES * HALF, N)
    return jnp.where(support == 1, image, density - BETA * image)


def first_kernel(density_ref, zh, zl, yh, yl, out_ref):
    send_forward(density_ref[...].reshape(PLANES * HALF, N), (zh, zl), (yh, yl), out_ref)


def middle_kernel(got_ref, support_ref, density_ref, iyh, iyl, izh, izl, zh, zl, yh, yl, field_ref, out_ref):
    field = updated(image_from(got_ref, (iyh, iyl), (izh, izl)), support_ref, density_ref)
    field_ref[...] = field.reshape(PLANES, HALF, N)
    send_forward(field, (zh, zl), (yh, yl), out_ref)


def last_kernel(got_ref, support_ref, density_ref, iyh, iyl, izh, izl, field_ref):
    field = updated(image_from(got_ref, (iyh, iyl), (izh, izl)), support_ref, density_ref)
    field_ref[...] = field.reshape(PLANES, HALF, N)


PACKET = jax.ShapeDtypeStruct((DEVS, 16, 128), jnp.float32)
FIELD = jax.ShapeDtypeStruct((PLANES, HALF, N), jnp.float32)


def first_field(density, t):
    return call(first_kernel, PACKET, in_specs=spec_vmem(5), out_specs=spec_vmem(1)[0])(
        density, *t["forward_z"], *t["forward_y"]
    )


def middle_field(got, support, density, t):
    return call(middle_kernel, (FIELD, PACKET), in_specs=spec_vmem(11), out_specs=tuple(spec_vmem(2)))(
        got, support, density, *t["inverse_y"], *t["inverse_z"], *t["forward_z"], *t["forward_y"]
    )


def last_field(got, support, density, t):
    return call(last_kernel, FIELD, in_specs=spec_vmem(7), out_specs=spec_vmem(1)[0])(
        got, support, density, *t["inverse_y"], *t["inverse_z"]
    )


def project_kernel(place_ref, got_ref, amplitude_ref, nyquist_ref, xh, xl, ixh, ixl, out_ref):
    first = place_ref[0]
    sign = place_ref[1].astype(jnp.float32)
    lanes = []
    for pm in range(2):
        parts = []
        for c in range(2):
            for x in range(PLANES):
                q = x * 4 + pm * 2 + c
                parts.append(got_ref[:SLABS, q, :] + sign * got_ref[SLABS:, q, :])
        lanes.append(jnp.concatenate(parts, axis=0))
    spectrum = table_times(xh[...], xl[...], jnp.concatenate(lanes, axis=1))
    real = spectrum[:N]
    imag = spectrum[N : 2 * N]
    mirror = spectrum[2 * N :]
    mirror = jnp.where(first == 1, mirror, jnp.concatenate([mirror[:, HALF:], mirror[:, :HALF]], axis=1))
    mirror_real = mirror[:N]
    mirror_imag = mirror[N:]
    amplitude = amplitude_ref[...]
    scale = amplitude * lax.rsqrt(real * real + imag * imag + SOFTEN)
    zero_real = 0.5 * (real + mirror_real)
    zero_imag = 0.5 * (imag - mirror_imag)
    top_real = 0.5 * (imag + mirror_imag)
    top_imag = 0.5 * (mirror_real - real)
    zero_scale = amplitude * lax.rsqrt(zero_real * zero_real + zero_imag * zero_imag + SOFTEN)
    top_scale = nyquist_ref[...] * lax.rsqrt(top_real * top_real + top_imag * top_imag + SOFTEN)
    packed = (lax.broadcasted_iota(jnp.int32, (N, N), 1) & (HALF - 1)) == 0
    new_real = jnp.where(packed, zero_scale * zero_real - top_scale * top_imag, scale * real)
    new_imag = jnp.where(packed, zero_scale * zero_imag + top_scale * top_real, scale * imag)
    result = table_times(ixh[...], ixl[...], jnp.concatenate([new_real, new_imag], axis=0))
    for pm in range(2):
        for c in range(2):
            for x in range(PLANES):
                q = x * 4 + pm * 2 + c
                start = (c * PLANES + x) * SLABS
                part = result[start : start + SLABS, pm * HALF : (pm + 1) * HALF]
                out_ref[:SLABS, q, :] = part
                out_ref[SLABS:, q, :] = sign * part


def projected(place, got, amplitude, nyquist, t):
    return call(project_kernel, PACKET, in_specs=[smem()] + spec_vmem(7), out_specs=spec_vmem(1)[0])(
        place, got, amplitude, nyquist, *t["forward_x"], *t["inverse_x"]
    )


def exchange(packet):
    sent = lax.all_to_all(packet.astype(jnp.float16), BOTH, split_axis=0, concat_axis=0, tiled=True)
    return sent.astype(jnp.float32)


def local(patterns, probabilities, source_row, target_row, support, density):
    t = tables()
    group = lax.axis_index("grp")
    device = group * SLABS + lax.axis_index("slab")
    place = jnp.stack([(device == 0).astype(jnp.int32), 1 - 2 * (device & 1)])

    got_field = exchange(first_field(density, t))

    block = probabilities[0]
    slices = jnp.einsum("kr,kp->rp", block, patterns[0], preferred_element_type=jnp.float32)
    rows = slices.astype(jnp.bfloat16).reshape(ROWS, 128)
    weight = jnp.sum(block.astype(jnp.float32), axis=0).astype(jnp.bfloat16).astype(jnp.float32)
    source = source_row[0, 0]
    send = gather_rows(
        weight,
        source.reshape(-1, 1),
        jnp.pad(source, ((0, 0), (0, 128 - CAP)), constant_values=-1),
        rows,
    )
    got = lax.all_to_all(send, "slab", split_axis=0, concat_axis=0, tiled=True)

    target = target_row[0, 0]
    zh = target & 1
    y = (target >> 1) & (N - 1)
    x = target >> 9
    pm = (y >= HALF).astype(jnp.int32)
    j = jnp.where(pm == 1, (N - y) & (HALF - 1), y)
    target = j * 16 + (pm * PLANES + x) * 2 + zh
    sums = place_rows(got, target.reshape(-1, 1), target.reshape(SLABS // OWNERS, 1, SLOTS))

    narrow = sums.astype(jnp.float16)
    got_sums = lax.all_to_all(narrow, BOTH, split_axis=0, concat_axis=0, tiled=True).astype(jnp.float32)
    theirs = lax.dynamic_slice_in_dim(narrow, (1 - group) * 8, 8, 1)
    other = lax.ppermute(jnp.concatenate([theirs, narrow[:, 16:]], axis=1), "grp", [(0, 1), (1, 0)])
    intensity = intensity_of(group.reshape(1), sums, other.astype(jnp.float32), t["flip_y"])

    amplitude, nyquist = amplitude_of(place, got_sums, t["flip_x"], t["flip_z"])
    back = exchange(projected(place, got_field, amplitude, nyquist, t))
    field, packet = middle_field(back, support, density, t)
    back = exchange(projected(place, exchange(packet), amplitude, nyquist, t))
    return (intensity, last_field(back, support, field, t))


def solution(mesh):
    return jax.shard_map(
        local,
        mesh=mesh,
        in_specs=(
            P("grp", "slab", None),
            P("grp", "slab", None),
            P("grp", "slab", None, None),
            P("grp", "slab", None, None),
            P("slab", "grp", None),
            P("slab", "grp", None),
        ),
        out_specs=(P("slab", "grp", None), P("slab", "grp", None)),
        check_vma=False,
    )
```

```python
import functools

import jax
import jax.numpy as jnp
import ml_dtypes
import numpy as np
from jax import lax
from jax.experimental import pallas as pl
from jax.experimental.pallas import tpu as pltpu
from jax.sharding import PartitionSpec as P

N = 256
HALF = N // 2
PLANES = 4
SLABS = 64
DEVS = 128
CAP = 80
ROWS = 4096
BETA = 0.9
SOFTEN = 0.25
BOTH = ("grp", "slab")
MIB = 1024 * 1024


def split_table(table):
    high = table.astype(np.float32).astype(ml_dtypes.bfloat16)
    low = (table - high.astype(np.float64)).astype(np.float32).astype(ml_dtypes.bfloat16)
    return (jnp.asarray(high), jnp.asarray(low))


def phase(rows, columns):
    angle = 2.0 * np.pi / N * ((rows[:, None] * columns[None, :]) % N)
    return (np.cos(angle) / np.sqrt(N), np.sin(angle) / np.sqrt(N))


@functools.cache
def tables():
    z = np.arange(N)
    cos, sin = phase(z, np.arange(HALF))
    nyquist = np.cos(np.pi * z) / np.sqrt(N)
    forward_z = np.concatenate([cos, -sin], axis=1)
    forward_z[:, HALF] = nyquist
    inverse_z = np.concatenate([2.0 * cos.T, -2.0 * sin.T], axis=0)
    inverse_z[0] = 1.0 / np.sqrt(N)
    inverse_z[HALF] = nyquist
    first = np.arange(DEVS)
    frequency = np.concatenate([first, np.where(first == 0, HALF, N - first)])
    cos_y, sin_y = phase(frequency, z)
    order = (np.arange(PLANES)[:, None] + PLANES * np.arange(SLABS)[None, :]).reshape(-1)
    cos_x, sin_x = phase(order, order)
    place = np.argsort(order)
    flips = np.zeros((3, N, N))
    flips[0, np.arange(N), place[(-order) % N]] = 1.0
    flips[1, (-z) % N, z] = 1.0
    flips[2, first, first] = 1.0
    flips[2, HALF + first, (-first) % HALF] = 1.0

    def split(parts):
        rows = []
        for part in parts:
            high = part.astype(np.float32).astype(ml_dtypes.bfloat16)
            rows += [high, (part - high.astype(np.float64)).astype(np.float32).astype(ml_dtypes.bfloat16)]
        return jnp.asarray(np.concatenate(rows, axis=0))

    return dict(
        forward=split([cos_y, sin_y, forward_z]),
        inverse=split([cos_y.T, sin_y.T, inverse_z]),
        slab=split([cos_x, sin_x]),
        flips=jnp.asarray(flips.astype(ml_dtypes.bfloat16)),
    )


def halves(values):
    high = values.astype(jnp.bfloat16)
    return (high, (values - high.astype(jnp.float32)).astype(jnp.bfloat16))


def dot(left, right):
    return jnp.dot(left, right, preferred_element_type=jnp.float32)


def table_left(ref, index, length=N):
    high = ref[2 * index * N : 2 * index * N + length]
    low = ref[(2 * index + 1) * N : (2 * index + 1) * N + length]
    return [high, low, high]


def times_table(values, ref, index):
    high, low = halves(values)
    top = ref[2 * index * N : (2 * index + 1) * N]
    rest = ref[(2 * index + 1) * N : (2 * index + 2) * N]
    return dot(jnp.concatenate([high, low, high], axis=1), jnp.concatenate([top, top, rest], axis=0))


def turn(ref, real, imag, sign, length=N):
    real = halves(real)
    imag = halves(imag)
    straight = [jnp.concatenate([a, b], axis=1) for a, b in zip(real, imag)]
    if sign > 0:
        crossed = [jnp.concatenate([-b, a], axis=1) for a, b in zip(real, imag)]
    else:
        crossed = [jnp.concatenate([b, -a], axis=1) for a, b in zip(real, imag)]
    left = jnp.concatenate(table_left(ref, 0, length) + table_left(ref, 1, length), axis=1)
    right = [straight[0], straight[0], straight[1], crossed[0], crossed[0], crossed[1]]
    return dot(left, jnp.concatenate(right, axis=0))


FINE = 2.0**14
OCTAVE = 32767.0 / 30.0
LOG2 = float(np.log(2.0))


def coded(values):
    size = jnp.minimum(jnp.log(1.0 + FINE * jnp.abs(values)) * (OCTAVE / LOG2), 32767.0)
    whole = (size + 0.5).astype(jnp.int32)
    return jnp.where(values < 0.0, -whole, whole).astype(jnp.int16)


def decoded(codes):
    values = codes.astype(jnp.int32).astype(jnp.float32)
    size = (jnp.exp(jnp.abs(values) * (LOG2 / OCTAVE)) - 1.0) * (1.0 / FINE)
    return jnp.where(values < 0.0, -size, size)


def call(kernel, out_shape, mib=16, **kwargs):
    return pl.pallas_call(
        kernel,
        out_shape=out_shape,
        compiler_params=pltpu.CompilerParams(vmem_limit_bytes=mib * MIB),
        **kwargs,
    )


def spec_vmem(count):
    return [pl.BlockSpec(memory_space=pltpu.VMEM)] * count


def smem():
    return pl.BlockSpec(memory_space=pltpu.SMEM)


def hbm():
    return pl.BlockSpec(memory_space=pltpu.HBM)


def fetch(source, target, sem):
    copy = pltpu.make_async_copy(source, target, sem)
    copy.start()
    return copy


BLOCKS = 4


def send_out(rows_ref, code_ref, out_ref, sems):
    count = code_ref.shape[1]
    copies = []
    for block in range(BLOCKS):
        devices = pl.ds(block * (DEVS // BLOCKS), DEVS // BLOCKS)
        code_ref[devices] = coded(rows_ref[devices, :count, :])
        copies.append(fetch(code_ref.at[devices], out_ref.at[devices], sems.at[block]))
    return copies


def table_scratch(rows):
    return pltpu.VMEM((rows, N), jnp.bfloat16)


def code_scratch(rows):
    return pltpu.VMEM((DEVS, rows, 128), jnp.int16)


def sems(count):
    return pltpu.SemaphoreType.DMA((count,))


CUTS = 8
CUT = DEVS // CUTS
EMPTY = 8
SEND = 88


def gather_kernel(index_ref, table_ref, probabilities_ref, patterns_ref, out_ref, block_ref, rows_ref, picked_ref, sem):
    def copy(cut):
        part = pl.ds(cut * CUT * 128, CUT * 128)
        return pltpu.make_async_copy(patterns_ref.at[:, part], block_ref.at[:, part], sem.at[cut])

    for cut in range(CUTS):
        copy(cut).start()
    rows_ref[:EMPTY] = jnp.zeros((EMPTY, 128), jnp.float32)
    turned = probabilities_ref[...].astype(jnp.float32).T
    left = turned.astype(jnp.bfloat16)
    for cut in range(CUTS):
        copy(cut).wait()
        part = dot(left, block_ref[:, cut * CUT * 128 : (cut + 1) * CUT * 128])
        part = part.astype(jnp.bfloat16).astype(jnp.float32)
        for d in range(CUT):
            rows_ref[pl.ds(EMPTY + cut * CUT + d, 32, stride=128), :] = part[:, d * 128 : (d + 1) * 128]

    def pick(step, unused):
        for o in range(2):
            owner = step * 2 + o
            for c in range(CAP):
                picked_ref[pl.ds(owner * CAP + c, 1), :] = rows_ref[pl.ds(EMPTY + index_ref[owner, c], 1), :]
        return unused

    lax.fori_loop(0, SLABS // 2, pick, 0)
    out_ref[:, :CAP, :] = picked_ref[...].astype(jnp.bfloat16).reshape(SLABS, CAP, 128)
    weight = jnp.sum(turned, axis=1, keepdims=True).astype(jnp.bfloat16).astype(jnp.float32)
    orientation = table_ref[...] >> 7
    weights = jnp.zeros((SLABS, CAP), jnp.float32)
    for r in range(32):
        weights = jnp.where(orientation == r, weight[r : r + 1], weights)
    weights = jnp.concatenate([weights, jnp.zeros((SLABS, 128 - CAP), jnp.float32)], axis=1)
    out_ref[:, CAP:, :] = jnp.broadcast_to(weights[:, None, :], (SLABS, 8, 128)).astype(jnp.bfloat16)


def gather_rows(source, probabilities, patterns):
    return call(
        gather_kernel,
        jax.ShapeDtypeStruct((SLABS, SEND, 128), jnp.bfloat16),
        mib=60,
        cost_estimate=pl.CostEstimate(flops=2 * 32 * 256 * 16384, bytes_accessed=32 * MIB, transcendentals=0),
        in_specs=[smem()] + spec_vmem(2) + [hbm()],
        out_specs=spec_vmem(1)[0],
        scratch_shapes=[
            pltpu.VMEM((256, DEVS * 128), jnp.bfloat16),
            pltpu.VMEM((EMPTY + ROWS, 128), jnp.float32),
            pltpu.VMEM((SLABS * CAP, 128), jnp.float32),
            pltpu.SemaphoreType.DMA((CUTS,)),
        ],
    )(source, source, probabilities, patterns)


SOURCES = 16
TAKEN = SOURCES * CAP
SLOTS = SLABS * CAP


def moved(target):
    y = (target >> 1) & (N - 1)
    pm = y >> 7
    j = jnp.where(pm == 1, (N - y) & (HALF - 1), y)
    return j * 16 + pm * 8 + (target >> 9) * 2 + (target & 1)


def columns_of(table):
    count = table.shape[0]
    square = jnp.concatenate([table, jnp.zeros((128 - count, 128), table.dtype)], axis=0).T
    return jnp.concatenate([square[:CAP, s : s + 1] for s in range(count)], axis=0)


def prepare_kernel(column_ref, out_ref, mark_ref, sem):
    copies = []
    for step in range(SLABS // SOURCES):
        slots = pl.ds(step * TAKEN, TAKEN)
        column = columns_of(moved(column_ref[step * SOURCES : (step + 1) * SOURCES]))
        mark = ((column >> 9) * 16 + (column & 15)).astype(jnp.float32)
        mark_ref[slots] = jnp.broadcast_to(mark, (TAKEN, 128)).astype(jnp.bfloat16)
        copies.append(fetch(mark_ref.at[slots], out_ref.at[slots], sem.at[step]))
    for copy in copies:
        copy.wait()


def prepare(column):
    return call(
        prepare_kernel,
        jax.ShapeDtypeStruct((SLOTS, 128), jnp.bfloat16),
        in_specs=spec_vmem(1),
        out_specs=hbm(),
        scratch_shapes=[pltpu.VMEM((SLOTS, 128), jnp.bfloat16), sems(SLABS // SOURCES)],
    )(column)


def place_kernel(got_ref, row_ref, mark_hbm, packet_ref, out_ref, sum_ref, mark_ref, code_ref, sem):
    steps = SLABS // SOURCES
    copies = []
    for step in range(steps):
        slots = pl.ds(step * TAKEN, TAKEN)
        copies.append(fetch(mark_hbm.at[slots], mark_ref.at[slots], sem.at[step]))
    code_ref[:, 24:, :] = packet_ref[...]
    weights = columns_of(got_ref[:, CAP:, :].astype(jnp.float32)[:, 0, :])
    total = jnp.zeros((DEVS, 128), jnp.float32)
    for step in range(steps):
        row = moved(row_ref[step])
        onehot = (lax.broadcasted_iota(jnp.int32, (512, TAKEN), 0) == (row & 511)).astype(jnp.bfloat16)
        left = (lax.broadcasted_iota(jnp.int32, (DEVS, TAKEN), 0) == (row >> 4)).astype(jnp.bfloat16)
        rows = got_ref[step * SOURCES : (step + 1) * SOURCES, :CAP].reshape(TAKEN, 128)
        copies[step].wait()
        mark = mark_ref[step * TAKEN : (step + 1) * TAKEN]
        zero = jnp.bfloat16(0)
        above = [rows] + [jnp.where(mark >= jnp.bfloat16(16 * q), rows, zero) for q in range(1, 4)]
        parts = [jnp.where(mark < jnp.bfloat16(16 * q + 16), above[q], zero) for q in range(3)] + [above[3]]
        part = dot(onehot, jnp.concatenate(parts, axis=1))
        sum_ref[...] = part if step == 0 else sum_ref[...] + part
        entry = mark.astype(jnp.float32).astype(jnp.int32) & 15
        lane = lax.broadcasted_iota(jnp.int32, (TAKEN, 128), 1)
        right = jnp.where(lane == entry, weights[step * TAKEN : (step + 1) * TAKEN], 0.0)
        total += dot(left, right.astype(jnp.bfloat16))
    total = coded(total)
    sent = []
    for q in range(4):
        devices = pl.ds(q * 32, 32)
        part = sum_ref[:, q * 128 : (q + 1) * 128].reshape(32, 16, 128)
        code_ref[devices, :16, :] = coded(part)
        code_ref[devices, 16:24, :] = jnp.broadcast_to(total[q * 32 : (q + 1) * 32][:, None, :], (32, 8, 128))
        sent.append(fetch(code_ref.at[devices], out_ref.at[devices], sem.at[q]))
    for copy in sent:
        copy.wait()


def place_rows(got, row, marks, packet):
    return call(
        place_kernel,
        jax.ShapeDtypeStruct((DEVS, 32, 128), jnp.int16),
        mib=28,
        in_specs=spec_vmem(2) + [hbm()] + spec_vmem(1),
        out_specs=hbm(),
        scratch_shapes=[
            pltpu.VMEM((512, 512), jnp.float32),
            pltpu.VMEM((SLOTS, 128), jnp.bfloat16),
            code_scratch(32),
            sems(4),
        ],
    )(got, row, marks, packet)


def intensity_kernel(group_ref, own_ref, other_ref, flip_ref, out_ref):
    group = group_ref[0]
    own = decoded(own_ref[:, :24, :])
    other = decoded(other_ref[...])
    total = jnp.where(group == 0, own[:, :8, :], own[:, 8:16, :]) + other[:, :8, :]
    weights = own[:, 16, :] + other[:, 8, :]
    divisor = jnp.maximum(jnp.where(group == 0, weights[:, :8], weights[:, 8:16]), 1.0)
    wide = jnp.concatenate([total[:, q, :] / divisor[:, q : q + 1] for q in range(8)], axis=1)
    flip = jnp.where(group == 0, flip_ref[2, :HALF, :HALF], flip_ref[2, HALF:, :HALF])
    high, low = halves(wide)
    turned = dot(flip, high) + dot(flip, low)
    for x in range(PLANES):
        out_ref[x] = turned[:, x * N : (x + 1) * N]


def intensity_of(group, own, other, flips):
    return call(
        intensity_kernel,
        jax.ShapeDtypeStruct((PLANES, HALF, N), jnp.float32),
        in_specs=[smem()] + spec_vmem(3),
        out_specs=pl.BlockSpec(memory_space=pltpu.VMEM),
    )(group, own, other, flips)


def amplitudes(first, got_ref, flip_ref):
    divisor = jnp.maximum(got_ref[:SLABS, 16, :] + got_ref[SLABS:, 16, :], 1.0)
    amplitude = []
    for pm in range(2):
        columns = []
        for zh in range(2):
            planes = []
            for x in range(PLANES):
                q = (pm * PLANES + x) * 2 + zh
                total = got_ref[:SLABS, q, :] + got_ref[SLABS:, q, :]
                planes.append(jnp.sqrt(total / divisor[:, q : q + 1]))
            columns.append(jnp.concatenate(planes, axis=0))
        amplitude.append(jnp.concatenate(columns, axis=1))
    mirrored = []
    for pm in range(2):
        high, low = halves(amplitude[pm])
        high = dot(flip_ref[0], high).astype(jnp.bfloat16)
        low = dot(flip_ref[0], low).astype(jnp.bfloat16)
        mirrored.append(dot(high, flip_ref[1]) + dot(low, flip_ref[1]))
    even = []
    for pm in range(2):
        partner = jnp.where(first == 1, mirrored[pm], mirrored[1 - pm])
        even.append(0.5 * (amplitude[pm] + partner))
    return (
        jnp.concatenate([part[:, :HALF] for part in even], axis=1),
        jnp.concatenate([part[:, HALF:] for part in even], axis=1),
    )


def tile(values, row, column):
    return values[row * 128 : (row + 1) * 128, column * 128 : (column + 1) * 128]


def send_forward(field, table_ref, rows_ref):
    partly = times_table(field, table_ref, 2)
    parts = []
    for c in range(2):
        parts.append(jnp.concatenate([partly[x * N : (x + 1) * N, c * HALF : (c + 1) * HALF] for x in range(2)], axis=1))
    result = turn(table_ref, parts[0], parts[1], -1)
    for x in range(2):
        for pm in range(2):
            for c in range(2):
                rows_ref[:, x * 4 + pm * 2 + c, :] = tile(result, pm, c * 2 + x)


def image_from(rows_ref, table_ref, length):
    planes = rows_ref.shape[1] // 4
    parts = []
    for c in range(2):
        columns = []
        for x in range(planes):
            columns.append(jnp.concatenate([rows_ref[:, x * 4 + pm * 2 + c, :] for pm in range(2)], axis=0))
        parts.append(jnp.concatenate(columns, axis=1))
    partly = turn(table_ref, parts[0], parts[1], 1, length)
    rows = []
    for x in range(planes):
        real = partly[:, x * HALF : (x + 1) * HALF]
        imag = partly[:, (planes + x) * HALF : (planes + x + 1) * HALF]
        rows.append(jnp.concatenate([real, imag], axis=1))
    return times_table(jnp.concatenate(rows, axis=0), table_ref, 2)


def first_kernel(density_ref, table_hbm, out_ref, rows_ref, table_ref, sem):
    fetch(table_hbm, table_ref, sem.at[0]).wait()
    send_forward(density_ref[...].reshape(2 * N, N), table_ref, rows_ref)
    out_ref[...] = coded(rows_ref[...])


def middle_kernel(
    got_ref, support_hbm, density_hbm, inverse_hbm, forward_hbm,
    field_hbm, code_hbm, out_ref,
    rows_ref, packet_ref, support_ref, density_ref, inverse_ref, forward_ref, field_ref, code_ref, sem,
):
    sources = ((inverse_hbm, inverse_ref), (support_hbm, support_ref), (density_hbm, density_ref), (forward_hbm, forward_ref))
    copies = [fetch(a, b, sem.at[i]) for i, (a, b) in enumerate(sources)]
    rows_ref[...] = decoded(got_ref[...])
    copies[0].wait()
    image = image_from(rows_ref, inverse_ref, N)
    copies[1].wait()
    copies[2].wait()
    support = support_ref[...].reshape(2 * N, N)
    density = density_ref[...].reshape(2 * N, N)
    field = jnp.where(support > 0.5, image, density - BETA * image)
    field_ref[...] = field.reshape(2, N, N)
    saved = [fetch(field_ref, field_hbm, sem.at[0])]
    copies[3].wait()
    send_forward(field, forward_ref, rows_ref)
    sent = send_out(rows_ref, packet_ref, out_ref, sem.at[pl.ds(4, BLOCKS)])
    code_ref[...] = coded(field_ref[...])
    saved.append(fetch(code_ref, code_hbm, sem.at[1]))
    for copy in sent + saved:
        copy.wait()


def last_kernel(
    group_ref, got_ref, support_hbm, own_hbm, other_ref, inverse_hbm,
    field_ref, rows_ref, support_ref, own_ref, inverse_ref, sem,
):
    group = group_ref[0]
    mine = own_hbm.at[:, pl.ds(pl.multiple_of(group * HALF, HALF), HALF), :]
    sources = ((inverse_hbm, inverse_ref), (support_hbm, support_ref), (mine, own_ref))
    copies = [fetch(a, b, sem.at[i]) for i, (a, b) in enumerate(sources)]
    rows_ref[...] = decoded(got_ref[...])
    copies[0].wait()
    image = image_from(rows_ref, inverse_ref, HALF).reshape(PLANES, HALF, N)
    other = decoded(other_ref[...])
    copies[1].wait()
    copies[2].wait()
    own = own_ref[...]
    for p in range(2):
        before = jnp.where(group == p, own, other)
        part = image[2 * p : 2 * p + 2]
        inside = support_ref[2 * p : 2 * p + 2] == 1
        field_ref[2 * p : 2 * p + 2] = jnp.where(inside, part, before - BETA * part)


PACKET = jax.ShapeDtypeStruct((DEVS, 8, 128), jnp.int16)
WIDE_PACKET = jax.ShapeDtypeStruct((DEVS, 16, 128), jnp.int16)


def scratch(rows):
    return pltpu.VMEM((DEVS, rows, 128), jnp.float32)


def first_field(density, t):
    return call(
        first_kernel,
        PACKET,
        in_specs=spec_vmem(1) + [hbm()],
        out_specs=spec_vmem(1)[0],
        scratch_shapes=[scratch(8), table_scratch(6 * N), sems(1)],
    )(density, t["forward"])


def middle_field(got, support, density, t):
    planes = (2, N, N)
    return call(
        middle_kernel,
        (jax.ShapeDtypeStruct(planes, jnp.float32), jax.ShapeDtypeStruct(planes, jnp.int16), PACKET),
        in_specs=spec_vmem(1) + [hbm()] * 4,
        out_specs=(hbm(),) * 3,
        scratch_shapes=[
            scratch(8),
            code_scratch(8),
            pltpu.VMEM(planes, jnp.float32),
            pltpu.VMEM(planes, jnp.float32),
            table_scratch(6 * N),
            table_scratch(6 * N),
            pltpu.VMEM(planes, jnp.float32),
            pltpu.VMEM(planes, jnp.int16),
            sems(4 + BLOCKS),
        ],
    )(got, support, density, t["inverse"], t["forward"])


def last_field(group, got, support, own, other, t):
    return call(
        last_kernel,
        jax.ShapeDtypeStruct((PLANES, HALF, N), jnp.float32),
        in_specs=[smem()] + spec_vmem(1) + [hbm()] * 2 + spec_vmem(1) + [hbm()],
        out_specs=spec_vmem(1)[0],
        scratch_shapes=[
            scratch(16),
            pltpu.VMEM((PLANES, HALF, N), jnp.int32),
            pltpu.VMEM((2, HALF, N), jnp.float32),
            table_scratch(6 * N),
            sems(3),
        ],
    )(group, got, support, own, other, t["inverse"])


def project(first, rows_ref, start, amplitude, nyquist, table_ref):
    lanes = []
    for c in range(2):
        for pm in range(2):
            parts = []
            for g in range(2):
                for x in range(2):
                    parts.append(rows_ref[g * SLABS : (g + 1) * SLABS, start + x * 4 + pm * 2 + c, :])
            lanes.append(jnp.concatenate(parts, axis=0))
    high, low = halves(jnp.concatenate(lanes, axis=1))
    right = jnp.concatenate([high, high, low], axis=0)
    by_cos = dot(jnp.concatenate(table_left(table_ref, 0), axis=1), right)
    by_sin = dot(jnp.concatenate(table_left(table_ref, 1), axis=1), right)
    real = by_cos[:, :N] + by_sin[:, N:]
    imag = by_cos[:, N:] - by_sin[:, :N]
    mirror_real = by_cos[:, :N] - by_sin[:, N:]
    mirror_imag = by_cos[:, N:] + by_sin[:, :N]

    def partner(mirror):
        return jnp.where(first == 1, mirror, jnp.concatenate([mirror[:, HALF:], mirror[:, :HALF]], axis=1))

    mirror_real = partner(mirror_real)
    mirror_imag = partner(mirror_imag)
    scale = amplitude * lax.rsqrt(real * real + imag * imag + SOFTEN)
    zero_real = 0.5 * (real + mirror_real)
    zero_imag = 0.5 * (imag - mirror_imag)
    top_real = 0.5 * (imag + mirror_imag)
    top_imag = 0.5 * (mirror_real - real)
    zero_scale = amplitude * lax.rsqrt(zero_real * zero_real + zero_imag * zero_imag + SOFTEN)
    top_scale = nyquist * lax.rsqrt(top_real * top_real + top_imag * top_imag + SOFTEN)
    packed = (lax.broadcasted_iota(jnp.int32, (N, N), 1) & (HALF - 1)) == 0
    new_real = jnp.where(packed, zero_scale * zero_real - top_scale * top_imag, scale * real)
    new_imag = jnp.where(packed, zero_scale * zero_imag + top_scale * top_real, scale * imag)
    return turn(table_ref, new_real, new_imag, 1)


def part_of(result, x, pm, c):
    lane = (c * 2 + pm) * HALF
    return result[x * SLABS : (x + 1) * SLABS, lane : lane + HALF]


def once_kernel(
    place_ref, got_ref, flip_hbm, table_hbm,
    out_ref, even_hbm,
    rows_ref, code_ref, flip_ref, table_ref, even_ref, sem,
):
    first = place_ref[0]
    copies = [fetch(flip_hbm, flip_ref, sem.at[0]), fetch(table_hbm, table_ref, sem.at[1])]
    rows_ref[...] = decoded(got_ref[...])
    copies[0].wait()
    amplitude, nyquist = amplitudes(first, rows_ref, flip_ref)
    even_ref[:N] = amplitude
    even_ref[N:] = nyquist
    saved = fetch(even_ref, even_hbm, sem.at[0])
    copies[1].wait()
    result = project(first, rows_ref, 24, amplitude, nyquist, table_ref)
    for pm in range(2):
        for c in range(2):
            for g in range(2):
                for x in range(2):
                    rows_ref[g * SLABS : (g + 1) * SLABS, x * 4 + pm * 2 + c, :] = part_of(result, g * 2 + x, pm, c)
    for copy in send_out(rows_ref, code_ref, out_ref, sem.at[pl.ds(2, BLOCKS)]) + [saved]:
        copy.wait()


def again_kernel(
    place_ref, got_ref, even_hbm, table_hbm,
    out_ref,
    rows_ref, code_ref, table_ref, even_ref, sem,
):
    sign = place_ref[1].astype(jnp.float32)
    copies = [fetch(table_hbm, table_ref, sem.at[0]), fetch(even_hbm, even_ref, sem.at[1])]
    rows_ref[:, :8, :] = decoded(got_ref[...])
    for copy in copies:
        copy.wait()
    result = project(place_ref[0], rows_ref, 0, even_ref[:N], even_ref[N:], table_ref)
    for pm in range(2):
        for c in range(2):
            for x in range(PLANES):
                q = x * 4 + pm * 2 + c
                part = part_of(result, x, pm, c)
                rows_ref[:SLABS, q, :] = part
                rows_ref[SLABS:, q, :] = sign * part
    for copy in send_out(rows_ref, code_ref, out_ref, sem.at[pl.ds(2, BLOCKS)]):
        copy.wait()


EVEN = jax.ShapeDtypeStruct((2 * N, N), jnp.float32)


def project_once(place, got, t):
    return call(
        once_kernel,
        (PACKET, EVEN),
        in_specs=[smem()] + spec_vmem(1) + [hbm()] * 2,
        out_specs=(hbm(), hbm()),
        scratch_shapes=[
            scratch(32),
            code_scratch(8),
            pltpu.VMEM((3, N, N), jnp.bfloat16),
            table_scratch(4 * N),
            pltpu.VMEM((2 * N, N), jnp.float32),
            sems(2 + BLOCKS),
        ],
    )(place, got, t["flips"], t["slab"])


def project_again(place, got, even, t):
    return call(
        again_kernel,
        WIDE_PACKET,
        in_specs=[smem()] + spec_vmem(1) + [hbm()] * 2,
        out_specs=hbm(),
        scratch_shapes=[
            scratch(16),
            code_scratch(16),
            table_scratch(4 * N),
            pltpu.VMEM((2 * N, N), jnp.float32),
            sems(2 + BLOCKS),
        ],
    )(place, got, even, t["slab"])


def exchange(packet):
    return lax.all_to_all(packet, BOTH, split_axis=0, concat_axis=0, tiled=True)


def swap(array):
    return lax.ppermute(array, "grp", [(0, 1), (1, 0)])


def local(patterns, probabilities, source_row, target_row, support, density):
    t = tables()
    group = lax.axis_index("grp")
    slab = lax.axis_index("slab")
    device = group * SLABS + slab
    place = jnp.stack([(device == 0).astype(jnp.int32), 1 - 2 * (device & 1)])
    pad = ((0, 0), (0, 128 - CAP))
    target = target_row[0, 0]

    fields = jnp.stack([density, support.astype(jnp.float32)])
    theirs = lax.dynamic_slice_in_dim(fields, 2 * (1 - group), 2, 1).astype(jnp.float16)
    other = swap(theirs)

    send = gather_rows(source_row[0, 0], probabilities[0], patterns[0])
    send, other = lax.optimization_barrier((send, other))
    got = lax.all_to_all(send, "slab", split_axis=0, concat_axis=0, tiled=True)

    own = lax.dynamic_slice_in_dim(fields, 2 * group, 2, 1)
    other = other.astype(jnp.float32)
    planes = jnp.concatenate([jnp.where(group == 0, own, other), jnp.where(group == 0, other, own)], axis=2)
    packet = first_field(planes[0], t)

    marks = prepare(jnp.pad(target, pad))
    sums = place_rows(got, target.reshape(SLABS // SOURCES, 1, TAKEN), marks, packet)
    got_sums = exchange(sums)

    theirs = lax.dynamic_slice_in_dim(sums, (1 - group) * 8, 8, 1)
    other = swap(jnp.concatenate([theirs, sums[:, 16:24]], axis=1))
    intensity = intensity_of(group.reshape(1), sums, other, t["flips"])

    packet, even = project_once(place, got_sums, t)
    field, code, packet = middle_field(exchange(packet), planes[1], planes[0], t)
    other = swap(lax.dynamic_slice_in_dim(code, (1 - group) * HALF, HALF, 1))
    got = exchange(project_again(place, exchange(packet), even, t))
    return (intensity, last_field(group.reshape(1), got, support, field, other, t))


def solution(mesh):
    return jax.shard_map(
        local,
        mesh=mesh,
        in_specs=(
            P("grp", "slab", None),
            P("grp", "slab", None),
            P("grp", "slab", None, None),
            P("grp", "slab", None, None),
            P("slab", "grp", None),
            P("slab", "grp", None),
        ),
        out_specs=(P("slab", "grp", None), P("slab", "grp", None)),
        check_vma=False,
    )
```

```python
import functools

import jax
import jax.numpy as jnp
import ml_dtypes
import numpy as np
from jax import lax
from jax.experimental import pallas as pl
from jax.experimental.pallas import tpu as pltpu
from jax.sharding import PartitionSpec as P

N = 256
HALF = N // 2
PLANES = 4
SLABS = 64
DEVS = 128
CAP = 80
ROWS = 4096
BETA = 0.9
SOFTEN = 0.25
BOTH = ("grp", "slab")
MIB = 1024 * 1024


def split_table(table):
    high = table.astype(np.float32).astype(ml_dtypes.bfloat16)
    low = (table - high.astype(np.float64)).astype(np.float32).astype(ml_dtypes.bfloat16)
    return (jnp.asarray(high), jnp.asarray(low))


def phase(rows, columns):
    angle = 2.0 * np.pi / N * ((rows[:, None] * columns[None, :]) % N)
    return (np.cos(angle) / np.sqrt(N), np.sin(angle) / np.sqrt(N))


@functools.cache
def tables():
    z = np.arange(N)
    cos, sin = phase(z, np.arange(HALF))
    nyquist = np.cos(np.pi * z) / np.sqrt(N)
    forward_z = np.concatenate([cos, -sin], axis=1)
    forward_z[:, HALF] = nyquist
    first = np.arange(DEVS)
    frequency = np.concatenate([first, np.where(first == 0, HALF, N - first)])
    cos_y, sin_y = phase(frequency, z)
    order = (np.arange(PLANES)[:, None] + PLANES * np.arange(SLABS)[None, :]).reshape(-1)
    cos_x, sin_x = phase(order, order)

    def split(parts):
        rows = []
        for part in parts:
            high = part.astype(np.float32).astype(ml_dtypes.bfloat16)
            rows += [high, (part - high.astype(np.float64)).astype(np.float32).astype(ml_dtypes.bfloat16)]
        return jnp.asarray(np.concatenate(rows, axis=0))

    return dict(field=split([cos_y, sin_y, forward_z]), slab=split([cos_x, sin_x]))


def halves(values):
    high = values.astype(jnp.bfloat16)
    return (high, (values - high.astype(jnp.float32)).astype(jnp.bfloat16))


def dot(left, right):
    return jnp.dot(left, right, preferred_element_type=jnp.float32)


def table_at(ref, index):
    high = ref[2 * index * N : (2 * index + 1) * N]
    low = ref[(2 * index + 1) * N : (2 * index + 2) * N]
    return [high, low, high]


def along_lanes(values, ref, index, back=False):
    high, low = halves(values)
    top, rest, unused = table_at(ref, index)
    left = jnp.concatenate([high, low, high], axis=1)
    if back:
        right = jnp.concatenate([top, top, rest], axis=1)
        return lax.dot_general(left, right, (((1,), (1,)), ((), ())), preferred_element_type=jnp.float32)
    return dot(left, jnp.concatenate([top, top, rest], axis=0))


def turn(ref, real, imag, sign, back=None):
    real = halves(real)
    imag = halves(imag)
    straight = [jnp.concatenate([a, b], axis=1) for a, b in zip(real, imag)]
    if sign > 0:
        crossed = [jnp.concatenate([-b, a], axis=1) for a, b in zip(real, imag)]
    else:
        crossed = [jnp.concatenate([b, -a], axis=1) for a, b in zip(real, imag)]
    left = table_at(ref, 0) + table_at(ref, 1)
    right = [straight[0], straight[0], straight[1], crossed[0], crossed[0], crossed[1]]
    right = jnp.concatenate(right, axis=0)
    if back is None:
        return dot(jnp.concatenate(left, axis=1), right)
    left = jnp.concatenate(left, axis=0)[:, :back]
    return lax.dot_general(left, right, (((0,), (0,)), ((), ())), preferred_element_type=jnp.float32)


def permutation(size, matches):
    row = lax.broadcasted_iota(jnp.int32, (size, size), 0)
    column = lax.broadcasted_iota(jnp.int32, (size, size), 1)
    return matches(row, column).astype(jnp.bfloat16)


FINE = 2.0**14
OCTAVE = 32767.0 / 30.0
LOG2 = float(np.log(2.0))


def coded(values):
    size = jnp.minimum(jnp.log(1.0 + FINE * jnp.abs(values)) * (OCTAVE / LOG2), 32767.0)
    whole = (size + 0.5).astype(jnp.int32)
    return jnp.where(values < 0.0, -whole, whole).astype(jnp.int16)


def decoded(codes):
    values = codes.astype(jnp.int32).astype(jnp.float32)
    size = (jnp.exp(jnp.abs(values) * (LOG2 / OCTAVE)) - 1.0) * (1.0 / FINE)
    return jnp.where(values < 0.0, -size, size)


def call(kernel, out_shape, mib=16, **kwargs):
    return pl.pallas_call(
        kernel,
        out_shape=out_shape,
        compiler_params=pltpu.CompilerParams(vmem_limit_bytes=mib * MIB),
        **kwargs,
    )


def spec_vmem(count):
    return [pl.BlockSpec(memory_space=pltpu.VMEM)] * count


def smem():
    return pl.BlockSpec(memory_space=pltpu.SMEM)


def hbm():
    return pl.BlockSpec(memory_space=pltpu.HBM)


def fetch(source, target, sem):
    copy = pltpu.make_async_copy(source, target, sem)
    copy.start()
    return copy


BLOCKS = 4


def send_out(rows_ref, code_ref, out_ref, sems):
    count = code_ref.shape[1]
    copies = []
    for block in range(BLOCKS):
        devices = pl.ds(block * (DEVS // BLOCKS), DEVS // BLOCKS)
        code_ref[devices] = coded(rows_ref[devices, :count, :])
        copies.append(fetch(code_ref.at[devices], out_ref.at[devices], sems.at[block]))
    return copies


def code_scratch(rows):
    return pltpu.VMEM((DEVS, rows, 128), jnp.int16)


def sems(count):
    return pltpu.SemaphoreType.DMA((count,))


CUTS = 8
CUT = DEVS // CUTS
EMPTY = 8
SEND = 88


def gather_kernel(
    index_ref, table_ref, probabilities_ref, patterns_ref, out_hbm, block_ref, rows_ref, picked_ref, out_ref, sem
):
    def copy(cut):
        part = pl.ds(cut * CUT * 128, CUT * 128)
        return pltpu.make_async_copy(patterns_ref.at[:, part], block_ref.at[:, part], sem.at[cut])

    for cut in range(CUTS):
        copy(cut).start()
    rows_ref[:EMPTY] = jnp.zeros((EMPTY, 128), jnp.float32)
    left = probabilities_ref[0]
    weight = jnp.sum(left.astype(jnp.float32), axis=1, keepdims=True).astype(jnp.bfloat16).astype(jnp.float32)
    orientation = table_ref[...] >> 7
    weights = jnp.zeros((SLABS, CAP), jnp.float32)
    for r in range(32):
        weights = jnp.where(orientation == r, weight[r : r + 1], weights)
    weights = jnp.concatenate([weights, jnp.zeros((SLABS, 128 - CAP), jnp.float32)], axis=1)
    out_ref[:, CAP:, :] = jnp.broadcast_to(weights[:, None, :], (SLABS, 8, 128)).astype(jnp.bfloat16)
    for cut in range(CUTS):
        copy(cut).wait()
        part = dot(left, block_ref[:, cut * CUT * 128 : (cut + 1) * CUT * 128])
        part = part.astype(jnp.bfloat16).astype(jnp.float32)
        for d in range(CUT):
            rows_ref[pl.ds(EMPTY + cut * CUT + d, 32, stride=128), :] = part[:, d * 128 : (d + 1) * 128]

    sent = []
    for part in range(BLOCKS):
        owners = SLABS // BLOCKS
        for o in range(part * owners, (part + 1) * owners):
            for c in range(CAP):
                picked_ref[o * CAP + c : o * CAP + c + 1, :] = rows_ref[pl.ds(EMPTY + index_ref[o, c], 1), :]
        picked = picked_ref[part * owners * CAP : (part + 1) * owners * CAP].astype(jnp.bfloat16)
        block = pl.ds(part * owners, owners)
        out_ref[block, :CAP, :] = picked.reshape(owners, CAP, 128)
        sent.append(fetch(out_ref.at[block], out_hbm.at[block], sem.at[part]))
    for copy in sent:
        copy.wait()


def gather_rows(source, probabilities, patterns):
    return call(
        gather_kernel,
        jax.ShapeDtypeStruct((SLABS, SEND, 128), jnp.bfloat16),
        mib=60,
        cost_estimate=pl.CostEstimate(flops=2 * 32 * 256 * 16384, bytes_accessed=32 * MIB, transcendentals=0),
        in_specs=[smem()] + spec_vmem(2) + [hbm()],
        out_specs=hbm(),
        scratch_shapes=[
            pltpu.VMEM((256, DEVS * 128), jnp.bfloat16),
            pltpu.VMEM((EMPTY + ROWS, 128), jnp.float32),
            pltpu.VMEM((SLABS * CAP, 128), jnp.float32),
            pltpu.VMEM((SLABS, SEND, 128), jnp.bfloat16),
            sems(CUTS),
        ],
    )(source, source, probabilities, patterns)


SOURCES = 16
TAKEN = SOURCES * CAP
SLOTS = SLABS * CAP


def moved(target):
    y = (target >> 1) & (N - 1)
    pm = y >> 7
    j = jnp.where(pm == 1, (N - y) & (HALF - 1), y)
    return j * 16 + pm * 8 + (target >> 9) * 2 + (target & 1)


def columns_of(table):
    count = table.shape[0]
    square = jnp.concatenate([table, jnp.zeros((128 - count, 128), table.dtype)], axis=0).T
    return jnp.concatenate([square[:CAP, s : s + 1] for s in range(count)], axis=0)


def place_kernel(got_ref, row_ref, column_ref, packet_ref, out_ref, sum_ref, code_ref, sem):
    steps = SLABS // SOURCES
    code_ref[:, 24:, :] = packet_ref[...]
    last = got_ref[:, CAP:, :].astype(jnp.float32)[:, 0, :]
    total = jnp.zeros((32, 128), jnp.float32)
    lane = lax.broadcasted_iota(jnp.int32, (TAKEN, 128), 1).astype(jnp.float32).astype(jnp.bfloat16)
    zero = jnp.bfloat16(0)
    for step in range(steps):
        row = moved(row_ref[step])
        onehot = (lax.broadcasted_iota(jnp.int32, (512, TAKEN), 0) == (row & 511)).astype(jnp.bfloat16)
        rows = got_ref[step * SOURCES : (step + 1) * SOURCES, :CAP].reshape(TAKEN, 128)
        column = moved(column_ref[step * SOURCES : (step + 1) * SOURCES])
        mark = columns_of((((column >> 9) * 16) + (column & 15)).astype(jnp.float32))
        mark = jnp.broadcast_to(mark, (TAKEN, 128)).astype(jnp.bfloat16)
        above = [rows] + [jnp.where(mark >= jnp.bfloat16(16 * q), rows, zero) for q in range(1, 4)]
        parts = [jnp.where(mark < jnp.bfloat16(16 * q + 16), above[q], zero) for q in range(3)] + [above[3]]
        part = dot(onehot, jnp.concatenate(parts, axis=1))
        sum_ref[...] = part if step == 0 else sum_ref[...] + part
        weights = [last[step * SOURCES + s : step * SOURCES + s + 1, :CAP] for s in range(SOURCES)]
        weights = jnp.concatenate(weights, axis=1)
        device = lax.broadcasted_iota(jnp.int32, (32, TAKEN), 0) == ((row >> 4) & 31)
        left = jnp.where(device, weights, 0.0).astype(jnp.bfloat16)
        total += dot(left, jnp.where(mark == lane, jnp.bfloat16(1), zero))
    total = coded(total).astype(jnp.int32)
    sent = []
    for q in range(4):
        devices = pl.ds(q * 32, 32)
        part = sum_ref[:, q * 128 : (q + 1) * 128].reshape(32, 16, 128)
        code_ref[devices, :16, :] = coded(part)
        entries = total if q == 0 else jnp.concatenate([total[:, 16 * q :], total[:, : 16 * q]], axis=1)
        code_ref[devices, 16:24, :] = jnp.broadcast_to(entries[:, None, :], (32, 8, 128)).astype(jnp.int16)
        sent.append(fetch(code_ref.at[devices], out_ref.at[devices], sem.at[q]))
    for copy in sent:
        copy.wait()


def place_rows(got, row, column, packet):
    return call(
        place_kernel,
        jax.ShapeDtypeStruct((DEVS, 32, 128), jnp.int16),
        mib=28,
        in_specs=spec_vmem(4),
        out_specs=hbm(),
        scratch_shapes=[
            pltpu.VMEM((512, 512), jnp.float32),
            code_scratch(32),
            sems(4),
        ],
    )(got, row, column, packet)


def intensity_kernel(group_ref, own_ref, other_ref, out_ref):
    group = group_ref[0]
    own = decoded(own_ref[:, :24, :])
    other = decoded(other_ref[...])
    total = jnp.where(group == 0, own[:, :8, :], own[:, 8:16, :]) + other[:, :8, :]
    weights = own[:, 16, :] + other[:, 8, :]
    divisor = jnp.maximum(jnp.where(group == 0, weights[:, :8], weights[:, 8:16]), 1.0)
    wide = jnp.concatenate([total[:, q, :] / divisor[:, q : q + 1] for q in range(8)], axis=1)
    same = permutation(HALF, lambda row, column: row == column)
    mirrored = permutation(HALF, lambda row, column: ((row + column) & (HALF - 1)) == 0)
    flip = jnp.where(group == 0, same, mirrored)
    high, low = halves(wide)
    turned = dot(flip, high) + dot(flip, low)
    for x in range(PLANES):
        out_ref[x] = turned[:, x * N : (x + 1) * N]


def intensity_of(group, own, other):
    return call(
        intensity_kernel,
        jax.ShapeDtypeStruct((PLANES, HALF, N), jnp.float32),
        in_specs=[smem()] + spec_vmem(2),
        out_specs=spec_vmem(1)[0],
    )(group, own, other)


def amplitudes(first, got_ref):
    scale = 1.0 / jnp.maximum(got_ref[:SLABS, 16, :] + got_ref[SLABS:, 16, :], 1.0)
    got_ref[:SLABS, :16, :] = got_ref[:SLABS, :16, :] + got_ref[SLABS:, :16, :]
    amplitude = []
    for pm in range(2):
        columns = []
        for zh in range(2):
            planes = []
            for x in range(PLANES):
                q = (pm * PLANES + x) * 2 + zh
                planes.append(jnp.sqrt(got_ref[:SLABS, q, :] * scale[:, q : q + 1]))
            columns.append(jnp.concatenate(planes, axis=0))
        amplitude.append(jnp.concatenate(columns, axis=1))
    flip_z = permutation(N, lambda row, column: ((row + column) & (N - 1)) == 0)

    def frequency(index):
        return PLANES * (index & (SLABS - 1)) + (index >> 6)

    flip_x = permutation(N, lambda row, column: ((frequency(row) + frequency(column)) & (N - 1)) == 0)
    mirrored = []
    for pm in range(2):
        high, low = halves(amplitude[pm])
        high = dot(flip_x, high).astype(jnp.bfloat16)
        low = dot(flip_x, low).astype(jnp.bfloat16)
        mirrored.append(dot(high, flip_z) + dot(low, flip_z))
    even = []
    for pm in range(2):
        partner = jnp.where(first == 1, mirrored[pm], mirrored[1 - pm])
        even.append(0.5 * (amplitude[pm] + partner))
    amplitude = jnp.concatenate([part[:, :HALF] for part in even], axis=1)
    return (
        jnp.where(packed_lanes(), amplitude, 2.0 * amplitude),
        jnp.concatenate([part[:, HALF:] for part in even], axis=1),
    )


def packed_lanes():
    return (lax.broadcasted_iota(jnp.int32, (N, N), 1) & (HALF - 1)) == 0


def tile(values, row, column):
    return values[row * 128 : (row + 1) * 128, column * 128 : (column + 1) * 128]


def send_forward(field, table_ref, rows_ref):
    partly = along_lanes(field, table_ref, 2)
    parts = []
    for c in range(2):
        parts.append(jnp.concatenate([partly[x * N : (x + 1) * N, c * HALF : (c + 1) * HALF] for x in range(2)], axis=1))
    result = turn(table_ref, parts[0], parts[1], -1)
    for x in range(2):
        for pm in range(2):
            for c in range(2):
                rows_ref[:, x * 4 + pm * 2 + c, :] = tile(result, pm, c * 2 + x)


def image_from(rows_ref, table_ref, length):
    planes = rows_ref.shape[1] // 4
    parts = []
    for c in range(2):
        columns = []
        for x in range(planes):
            columns.append(jnp.concatenate([rows_ref[:, x * 4 + pm * 2 + c, :] for pm in range(2)], axis=0))
        parts.append(jnp.concatenate(columns, axis=1))
    partly = turn(table_ref, parts[0], parts[1], 1, length)
    rows = []
    for x in range(planes):
        real = partly[:, x * HALF : (x + 1) * HALF]
        imag = partly[:, (planes + x) * HALF : (planes + x + 1) * HALF]
        rows.append(jnp.concatenate([real, imag], axis=1))
    return along_lanes(jnp.concatenate(rows, axis=0), table_ref, 2, True)


def updated(rows_ref, support_ref, density_ref, table_ref):
    image = image_from(rows_ref, table_ref, N)
    support = support_ref[...].reshape(2 * N, N)
    density = density_ref[...].reshape(2 * N, N)
    return jnp.where(support == 1, image, density - BETA * image)


def first_kernel(density_ref, table_ref, out_ref, rows_ref):
    send_forward(density_ref[...].reshape(2 * N, N), table_ref, rows_ref)
    out_ref[...] = coded(rows_ref[...])


def middle_kernel(got_ref, support_ref, density_ref, table_ref, out_ref, rows_ref, code_ref, sem):
    rows_ref[...] = decoded(got_ref[...])
    field = updated(rows_ref, support_ref, density_ref, table_ref)
    send_forward(field, table_ref, rows_ref)
    for copy in send_out(rows_ref, code_ref, out_ref, sem):
        copy.wait()


def keep_kernel(group_ref, got_ref, support_ref, density_ref, table_ref, own_ref, code_ref, rows_ref, field_ref):
    group = group_ref[0]
    rows_ref[...] = decoded(got_ref[...])
    field_ref[...] = updated(rows_ref, support_ref, density_ref, table_ref).reshape(2, N, N)
    own_ref[...] = field_ref[:, pl.ds(pl.multiple_of(group * HALF, HALF), HALF), :]
    code_ref[...] = coded(field_ref[:, pl.ds(pl.multiple_of((1 - group) * HALF, HALF), HALF), :])


def last_kernel(group_ref, got_ref, support_ref, own_ref, other_ref, table_ref, field_ref, rows_ref):
    group = group_ref[0]
    rows_ref[...] = decoded(got_ref[...])
    image = image_from(rows_ref, table_ref, HALF).reshape(PLANES, HALF, N)
    other = decoded(other_ref[...])
    own = own_ref[...]
    for p in range(2):
        before = jnp.where(group == p, own, other)
        part = image[2 * p : 2 * p + 2]
        inside = support_ref[2 * p : 2 * p + 2] == 1
        field_ref[2 * p : 2 * p + 2] = jnp.where(inside, part, before - BETA * part)


PACKET = jax.ShapeDtypeStruct((DEVS, 8, 128), jnp.int16)
WIDE_PACKET = jax.ShapeDtypeStruct((DEVS, 16, 128), jnp.int16)


def scratch(rows):
    return pltpu.VMEM((DEVS, rows, 128), jnp.float32)


def first_field(density, t):
    return call(
        first_kernel, PACKET, in_specs=spec_vmem(2), out_specs=spec_vmem(1)[0], scratch_shapes=[scratch(8)]
    )(density, t["field"])


def middle_field(got, support, density, t):
    return call(
        middle_kernel,
        PACKET,
        in_specs=spec_vmem(4),
        out_specs=hbm(),
        scratch_shapes=[scratch(8), code_scratch(8), sems(BLOCKS)],
    )(got, support, density, t["field"])


def kept_field(group, got, support, density, t):
    shape = (2, HALF, N)
    return call(
        keep_kernel,
        (jax.ShapeDtypeStruct(shape, jnp.float32), jax.ShapeDtypeStruct(shape, jnp.int16)),
        in_specs=[smem()] + spec_vmem(4),
        out_specs=tuple(spec_vmem(2)),
        scratch_shapes=[scratch(8), pltpu.VMEM((2, N, N), jnp.float32)],
    )(group, got, support, density, t["field"])


def last_field(group, got, support, own, other, t):
    return call(
        last_kernel,
        jax.ShapeDtypeStruct((PLANES, HALF, N), jnp.float32),
        in_specs=[smem()] + spec_vmem(5),
        out_specs=spec_vmem(1)[0],
        scratch_shapes=[scratch(16)],
    )(group, got, support, own, other, t["field"])


def project(first, rows_ref, start, amplitude, nyquist, table_ref):
    lanes = []
    for c in range(2):
        for pm in range(2):
            parts = []
            for g in range(2):
                for x in range(2):
                    parts.append(rows_ref[g * SLABS : (g + 1) * SLABS, start + x * 4 + pm * 2 + c, :])
            lanes.append(jnp.concatenate(parts, axis=0))
    high, low = halves(jnp.concatenate(lanes, axis=1))
    right = jnp.concatenate([high, high, low], axis=0)
    by_cos = dot(jnp.concatenate(table_at(table_ref, 0), axis=1), right)
    by_sin = dot(jnp.concatenate(table_at(table_ref, 1), axis=1), right)
    real = by_cos[:, :N] + by_sin[:, N:]
    imag = by_cos[:, N:] - by_sin[:, :N]
    mirror_real = by_cos[:, :N] - by_sin[:, N:]
    mirror_imag = by_cos[:, N:] + by_sin[:, :N]

    def partner(mirror):
        return jnp.where(first == 1, mirror, jnp.concatenate([mirror[:, HALF:], mirror[:, :HALF]], axis=1))

    mirror_real = partner(mirror_real)
    mirror_imag = partner(mirror_imag)
    scale = amplitude * lax.rsqrt(real * real + imag * imag + SOFTEN)
    zero_real = 0.5 * (real + mirror_real)
    zero_imag = 0.5 * (imag - mirror_imag)
    top_real = 0.5 * (imag + mirror_imag)
    top_imag = 0.5 * (mirror_real - real)
    zero_scale = amplitude * lax.rsqrt(zero_real * zero_real + zero_imag * zero_imag + SOFTEN)
    top_scale = nyquist * lax.rsqrt(top_real * top_real + top_imag * top_imag + SOFTEN)
    packed = packed_lanes()
    new_real = jnp.where(packed, zero_scale * zero_real - top_scale * top_imag, scale * real)
    new_imag = jnp.where(packed, zero_scale * zero_imag + top_scale * top_real, scale * imag)
    return turn(table_ref, new_real, new_imag, 1)


def part_of(result, x, pm, c):
    lane = (c * 2 + pm) * HALF
    return result[x * SLABS : (x + 1) * SLABS, lane : lane + HALF]


def once_kernel(place_ref, got_ref, table_ref, out_ref, rows_ref, code_ref, sem):
    first = place_ref[0]
    rows_ref[...] = decoded(got_ref[...])
    amplitude, nyquist = amplitudes(first, rows_ref)
    result = project(first, rows_ref, 24, amplitude, nyquist, table_ref)
    for pm in range(2):
        for c in range(2):
            for g in range(2):
                for x in range(2):
                    rows_ref[g * SLABS : (g + 1) * SLABS, x * 4 + pm * 2 + c, :] = part_of(result, g * 2 + x, pm, c)
    for copy in send_out(rows_ref, code_ref, out_ref, sem):
        copy.wait()


def even_kernel(place_ref, got_ref, even_ref, rows_ref):
    rows_ref[...] = decoded(got_ref[:, :24, :])
    amplitude, nyquist = amplitudes(place_ref[0], rows_ref)
    even_ref[:N] = amplitude
    even_ref[N:] = nyquist


def again_kernel(
    place_ref, got_ref, even_ref, table_ref, out_hbm, rows_ref, code_ref, sem
):
    sign = place_ref[1]
    rows_ref[:, :8, :] = decoded(got_ref[...])
    result = project(place_ref[0], rows_ref, 0, even_ref[:N], even_ref[N:], table_ref)
    for pm in range(2):
        for c in range(2):
            for x in range(PLANES):
                rows_ref[:SLABS, x * 4 + pm * 2 + c, :] = part_of(result, x, pm, c)
    sent = []
    for block in range(2):
        slabs = pl.ds(block * 32, 32)
        others = pl.ds(SLABS + block * 32, 32)
        codes = coded(rows_ref[slabs]).astype(jnp.int32)
        code_ref[slabs] = codes.astype(jnp.int16)
        code_ref[others] = (sign * codes).astype(jnp.int16)
        sent.append(fetch(code_ref.at[slabs], out_hbm.at[slabs], sem.at[2 * block]))
        sent.append(fetch(code_ref.at[others], out_hbm.at[others], sem.at[2 * block + 1]))
    for copy in sent:
        copy.wait()


EVEN = jax.ShapeDtypeStruct((2 * N, N), jnp.float32)


def project_once(place, got, t):
    return call(
        once_kernel,
        PACKET,
        in_specs=[smem()] + spec_vmem(2),
        out_specs=hbm(),
        scratch_shapes=[scratch(32), code_scratch(8), sems(BLOCKS)],
    )(place, got, t["slab"])


def kept_amplitude(place, got):
    return call(
        even_kernel, EVEN, in_specs=[smem()] + spec_vmem(1), out_specs=spec_vmem(1)[0], scratch_shapes=[scratch(24)]
    )(place, got)


def project_again(place, got, even, t):
    return call(
        again_kernel,
        WIDE_PACKET,
        in_specs=[smem()] + spec_vmem(3),
        out_specs=hbm(),
        scratch_shapes=[scratch(16), code_scratch(16), sems(BLOCKS)],
    )(place, got, even, t["slab"])


def exchange(packet):
    return lax.all_to_all(packet, BOTH, split_axis=0, concat_axis=0, tiled=True)


def swap(array):
    return lax.ppermute(array, "grp", [(0, 1), (1, 0)])


def local(patterns, probabilities, source_row, target_row, support, density):
    t = tables()
    group = lax.axis_index("grp")
    slab = lax.axis_index("slab")
    device = group * SLABS + slab
    place = jnp.stack([(device == 0).astype(jnp.int32), 1 - 2 * (device & 1)])
    pad = ((0, 0), (0, 128 - CAP))
    target = target_row[0, 0]

    send = gather_rows(source_row[0, 0], jnp.swapaxes(probabilities, 1, 2), patterns[0])
    got = lax.all_to_all(send, "slab", split_axis=0, concat_axis=0, tiled=True)

    def whole(field, kind):
        other = swap(lax.dynamic_slice_in_dim(field, 2 * (1 - group), 2, 0).astype(kind)).astype(field.dtype)
        own = lax.dynamic_slice_in_dim(field, 2 * group, 2, 0)
        return jnp.concatenate([jnp.where(group == 0, own, other), jnp.where(group == 0, other, own)], axis=1)

    planes = whole(density, jnp.float16)
    packet = first_field(planes, t)
    sums = place_rows(got, target.reshape(SLABS // SOURCES, 1, TAKEN), jnp.pad(target, pad), packet)
    late, sums = lax.optimization_barrier((support, sums))
    got_sums = exchange(sums)
    inside = whole(late, jnp.int16)

    theirs = lax.dynamic_slice_in_dim(sums, (1 - group) * 8, 8, 1)
    other = swap(jnp.concatenate([theirs, sums[:, 16:24]], axis=1))
    intensity = intensity_of(group.reshape(1), sums, other)

    back = exchange(project_once(place, got_sums, t))
    back, even, inside = lax.optimization_barrier((back, kept_amplitude(place, got_sums), inside))
    got = exchange(middle_field(back, inside, planes, t))
    own, theirs = kept_field(group.reshape(1), back, inside, planes, t)
    got, own, other = lax.optimization_barrier((got, own, swap(theirs)))
    back = exchange(project_again(place, got, even, t))
    return (intensity, last_field(group.reshape(1), back, support, own, other, t))


def solution(mesh):
    return jax.shard_map(
        local,
        mesh=mesh,
        in_specs=(
            P("grp", "slab", None),
            P("grp", "slab", None),
            P("grp", "slab", None, None),
            P("grp", "slab", None, None),
            P("slab", "grp", None),
            P("slab", "grp", None),
        ),
        out_specs=(P("slab", "grp", None), P("slab", "grp", None)),
        check_vma=False,
    )
```

```python
import functools

import jax
import jax.numpy as jnp
import ml_dtypes
import numpy as np
from jax import lax
from jax.experimental import pallas as pl
from jax.experimental.pallas import tpu as pltpu
from jax.sharding import PartitionSpec as P

N = 256
HALF = N // 2
PLANES = 4
SLABS = 64
DEVS = 128
CAP = 80
ROWS = 4096
BETA = 0.9
SOFTEN = 0.25
BOTH = ("grp", "slab")
MIB = 1024 * 1024


def split_table(table):
    high = table.astype(np.float32).astype(ml_dtypes.bfloat16)
    low = (table - high.astype(np.float64)).astype(np.float32).astype(ml_dtypes.bfloat16)
    return (jnp.asarray(high), jnp.asarray(low))


def phase(rows, columns):
    angle = 2.0 * np.pi / N * ((rows[:, None] * columns[None, :]) % N)
    return (np.cos(angle) / np.sqrt(N), np.sin(angle) / np.sqrt(N))


@functools.cache
def tables():
    z = np.arange(N)
    cos, sin = phase(z, np.arange(HALF))
    nyquist = np.cos(np.pi * z) / np.sqrt(N)
    forward_z = np.concatenate([cos, -sin], axis=1)
    forward_z[:, HALF] = nyquist
    first = np.arange(DEVS)
    frequency = np.concatenate([first, np.where(first == 0, HALF, N - first)])
    cos_y, sin_y = phase(frequency, z)
    order = (np.arange(PLANES)[:, None] + PLANES * np.arange(SLABS)[None, :]).reshape(-1)
    cos_x, sin_x = phase(order, order)

    def split(parts):
        rows = []
        for part in parts:
            high = part.astype(np.float32).astype(ml_dtypes.bfloat16)
            rows += [high, (part - high.astype(np.float64)).astype(np.float32).astype(ml_dtypes.bfloat16)]
        return jnp.asarray(np.concatenate(rows, axis=0))

    return dict(field=split([cos_y, sin_y, forward_z]), slab=split([cos_x, sin_x]))


def halves(values):
    high = values.astype(jnp.bfloat16)
    return (high, (values - high.astype(jnp.float32)).astype(jnp.bfloat16))


def dot(left, right):
    return jnp.dot(left, right, preferred_element_type=jnp.float32)


def table_at(ref, index):
    high = ref[2 * index * N : (2 * index + 1) * N]
    low = ref[(2 * index + 1) * N : (2 * index + 2) * N]
    return [high, low, high]


def along_lanes(values, ref, index, back=False):
    high, low = halves(values)
    top, rest, unused = table_at(ref, index)
    left = jnp.concatenate([high, low, high], axis=1)
    if back:
        right = jnp.concatenate([top, top, rest], axis=1)
        return lax.dot_general(left, right, (((1,), (1,)), ((), ())), preferred_element_type=jnp.float32)
    return dot(left, jnp.concatenate([top, top, rest], axis=0))


def turn(ref, real, imag, sign, back=None):
    real = halves(real)
    imag = halves(imag)
    straight = [jnp.concatenate([a, b], axis=1) for a, b in zip(real, imag)]
    if sign > 0:
        crossed = [jnp.concatenate([-b, a], axis=1) for a, b in zip(real, imag)]
    else:
        crossed = [jnp.concatenate([b, -a], axis=1) for a, b in zip(real, imag)]
    left = table_at(ref, 0) + table_at(ref, 1)
    right = [straight[0], straight[0], straight[1], crossed[0], crossed[0], crossed[1]]
    right = jnp.concatenate(right, axis=0)
    if back is None:
        return dot(jnp.concatenate(left, axis=1), right)
    left = jnp.concatenate(left, axis=0)[:, :back]
    return lax.dot_general(left, right, (((0,), (0,)), ((), ())), preferred_element_type=jnp.float32)


def permutation(size, matches):
    row = lax.broadcasted_iota(jnp.int32, (size, size), 0)
    column = lax.broadcasted_iota(jnp.int32, (size, size), 1)
    return matches(row, column).astype(jnp.bfloat16)


FINE = 2.0**14
OCTAVE = 32767.0 / 30.0
LOG2 = float(np.log(2.0))


def coded(values):
    size = jnp.minimum(jnp.log(1.0 + FINE * jnp.abs(values)) * (OCTAVE / LOG2), 32767.0)
    whole = (size + 0.5).astype(jnp.int32)
    return jnp.where(values < 0.0, -whole, whole).astype(jnp.int16)


def decoded(codes):
    values = codes.astype(jnp.int32).astype(jnp.float32)
    size = (jnp.exp(jnp.abs(values) * (LOG2 / OCTAVE)) - 1.0) * (1.0 / FINE)
    return jnp.where(values < 0.0, -size, size)


def call(kernel, out_shape, mib=16, **kwargs):
    return pl.pallas_call(
        kernel,
        out_shape=out_shape,
        compiler_params=pltpu.CompilerParams(vmem_limit_bytes=mib * MIB),
        **kwargs,
    )


def spec_vmem(count):
    return [pl.BlockSpec(memory_space=pltpu.VMEM)] * count


def smem():
    return pl.BlockSpec(memory_space=pltpu.SMEM)


def hbm():
    return pl.BlockSpec(memory_space=pltpu.HBM)


def fetch(source, target, sem):
    copy = pltpu.make_async_copy(source, target, sem)
    copy.start()
    return copy


BLOCKS = 4


def send_out(rows_ref, code_ref, out_ref, sems):
    count = code_ref.shape[1]
    copies = []
    for block in range(BLOCKS):
        devices = pl.ds(block * (DEVS // BLOCKS), DEVS // BLOCKS)
        code_ref[devices] = coded(rows_ref[devices, :count, :])
        copies.append(fetch(code_ref.at[devices], out_ref.at[devices], sems.at[block]))
    return copies


def code_scratch(rows):
    return pltpu.VMEM((DEVS, rows, 128), jnp.int16)


def sems(count):
    return pltpu.SemaphoreType.DMA((count,))


CUTS = 8
CUT = DEVS // CUTS
EMPTY = 8
SEND = 88


def gather_kernel(
    index_ref, table_ref, probabilities_ref, patterns_ref, out_hbm, block_ref, rows_ref, picked_ref, out_ref, sem
):
    def copy(cut):
        part = pl.ds(cut * CUT * 128, CUT * 128)
        return pltpu.make_async_copy(patterns_ref.at[:, part], block_ref.at[:, part], sem.at[cut])

    for cut in range(CUTS):
        copy(cut).start()
    rows_ref[:EMPTY] = jnp.zeros((EMPTY, 128), jnp.float32)
    left = probabilities_ref[0]
    weight = jnp.sum(left.astype(jnp.float32), axis=1, keepdims=True).astype(jnp.bfloat16).astype(jnp.float32)
    orientation = table_ref[...] >> 7
    weights = jnp.zeros((SLABS, CAP), jnp.float32)
    for r in range(32):
        weights = jnp.where(orientation == r, weight[r : r + 1], weights)
    weights = jnp.concatenate([weights, jnp.zeros((SLABS, 128 - CAP), jnp.float32)], axis=1)
    out_ref[:, CAP:, :] = jnp.broadcast_to(weights[:, None, :], (SLABS, 8, 128)).astype(jnp.bfloat16)
    for cut in range(CUTS):
        copy(cut).wait()
        part = dot(left, block_ref[:, cut * CUT * 128 : (cut + 1) * CUT * 128])
        part = part.astype(jnp.bfloat16).astype(jnp.float32)
        for d in range(CUT):
            rows_ref[pl.ds(EMPTY + cut * CUT + d, 32, stride=128), :] = part[:, d * 128 : (d + 1) * 128]

    sent = []
    for part in range(BLOCKS):
        owners = SLABS // BLOCKS
        for o in range(part * owners, (part + 1) * owners):
            for c in range(CAP):
                picked_ref[o * CAP + c : o * CAP + c + 1, :] = rows_ref[pl.ds(EMPTY + index_ref[o, c], 1), :]
        picked = picked_ref[part * owners * CAP : (part + 1) * owners * CAP].astype(jnp.bfloat16)
        block = pl.ds(part * owners, owners)
        out_ref[block, :CAP, :] = picked.reshape(owners, CAP, 128)
        sent.append(fetch(out_ref.at[block], out_hbm.at[block], sem.at[part]))
    for copy in sent:
        copy.wait()


def gather_rows(source, probabilities, patterns):
    return call(
        gather_kernel,
        jax.ShapeDtypeStruct((SLABS, SEND, 128), jnp.bfloat16),
        mib=60,
        cost_estimate=pl.CostEstimate(flops=2 * 32 * 256 * 16384, bytes_accessed=32 * MIB, transcendentals=0),
        in_specs=[smem()] + spec_vmem(2) + [hbm()],
        out_specs=hbm(),
        scratch_shapes=[
            pltpu.VMEM((256, DEVS * 128), jnp.bfloat16),
            pltpu.VMEM((EMPTY + ROWS, 128), jnp.float32),
            pltpu.VMEM((SLABS * CAP, 128), jnp.float32),
            pltpu.VMEM((SLABS, SEND, 128), jnp.bfloat16),
            sems(CUTS),
        ],
    )(source, source, probabilities, patterns)


SOURCES = 16
TAKEN = SOURCES * CAP
SLOTS = SLABS * CAP


def moved(target):
    y = (target >> 1) & (N - 1)
    pm = y >> 7
    j = jnp.where(pm == 1, (N - y) & (HALF - 1), y)
    return j * 16 + pm * 8 + (target >> 9) * 2 + (target & 1)


def columns_of(table):
    count = table.shape[0]
    square = jnp.concatenate([table, jnp.zeros((128 - count, 128), table.dtype)], axis=0).T
    return jnp.concatenate([square[:CAP, s : s + 1] for s in range(count)], axis=0)


def place_kernel(got_ref, row_ref, column_ref, packet_ref, out_ref, sum_ref, code_ref, sem):
    steps = SLABS // SOURCES
    code_ref[:, 24:, :] = packet_ref[...]
    last = got_ref[:, CAP:, :].astype(jnp.float32)[:, 0, :]
    total = jnp.zeros((32, 128), jnp.float32)
    lane = lax.broadcasted_iota(jnp.int32, (TAKEN, 128), 1).astype(jnp.float32).astype(jnp.bfloat16)
    zero = jnp.bfloat16(0)
    for step in range(steps):
        row = moved(row_ref[step])
        onehot = (lax.broadcasted_iota(jnp.int32, (512, TAKEN), 0) == (row & 511)).astype(jnp.bfloat16)
        rows = got_ref[step * SOURCES : (step + 1) * SOURCES, :CAP].reshape(TAKEN, 128)
        column = moved(column_ref[step * SOURCES : (step + 1) * SOURCES])
        mark = columns_of((((column >> 9) * 16) + (column & 15)).astype(jnp.float32))
        mark = jnp.broadcast_to(mark, (TAKEN, 128)).astype(jnp.bfloat16)
        above = [rows] + [jnp.where(mark >= jnp.bfloat16(16 * q), rows, zero) for q in range(1, 4)]
        parts = [jnp.where(mark < jnp.bfloat16(16 * q + 16), above[q], zero) for q in range(3)] + [above[3]]
        part = dot(onehot, jnp.concatenate(parts, axis=1))
        sum_ref[...] = part if step == 0 else sum_ref[...] + part
        weights = [last[step * SOURCES + s : step * SOURCES + s + 1, :CAP] for s in range(SOURCES)]
        weights = jnp.concatenate(weights, axis=1)
        device = lax.broadcasted_iota(jnp.int32, (32, TAKEN), 0) == ((row >> 4) & 31)
        left = jnp.where(device, weights, 0.0).astype(jnp.bfloat16)
        total += dot(left, jnp.where(mark == lane, jnp.bfloat16(1), zero))
    total = coded(total).astype(jnp.int32)
    sent = []
    for q in range(4):
        devices = pl.ds(q * 32, 32)
        part = sum_ref[:, q * 128 : (q + 1) * 128].reshape(32, 16, 128)
        code_ref[devices, :16, :] = coded(part)
        entries = total if q == 0 else jnp.concatenate([total[:, 16 * q :], total[:, : 16 * q]], axis=1)
        code_ref[devices, 16:24, :] = jnp.broadcast_to(entries[:, None, :], (32, 8, 128)).astype(jnp.int16)
        sent.append(fetch(code_ref.at[devices], out_ref.at[devices], sem.at[q]))
    for copy in sent:
        copy.wait()


def place_rows(got, row, column, packet):
    return call(
        place_kernel,
        jax.ShapeDtypeStruct((DEVS, 32, 128), jnp.int16),
        mib=28,
        in_specs=spec_vmem(4),
        out_specs=hbm(),
        scratch_shapes=[
            pltpu.VMEM((512, 512), jnp.float32),
            code_scratch(32),
            sems(4),
        ],
    )(got, row, column, packet)


def intensity_kernel(group_ref, own_ref, other_ref, out_ref):
    group = group_ref[0]
    own = decoded(own_ref[:, :24, :])
    other = decoded(other_ref[...])
    total = jnp.where(group == 0, own[:, :8, :], own[:, 8:16, :]) + other[:, :8, :]
    weights = own[:, 16, :] + other[:, 8, :]
    divisor = jnp.maximum(jnp.where(group == 0, weights[:, :8], weights[:, 8:16]), 1.0)
    wide = jnp.concatenate([total[:, q, :] / divisor[:, q : q + 1] for q in range(8)], axis=1)
    same = permutation(HALF, lambda row, column: row == column)
    mirrored = permutation(HALF, lambda row, column: ((row + column) & (HALF - 1)) == 0)
    flip = jnp.where(group == 0, same, mirrored)
    high, low = halves(wide)
    turned = dot(flip, high) + dot(flip, low)
    for x in range(PLANES):
        out_ref[x] = turned[:, x * N : (x + 1) * N]


def intensity_of(group, own, other):
    return call(
        intensity_kernel,
        jax.ShapeDtypeStruct((PLANES, HALF, N), jnp.float32),
        in_specs=[smem()] + spec_vmem(2),
        out_specs=spec_vmem(1)[0],
    )(group, own, other)


def amplitudes(first, got_ref):
    scale = 1.0 / jnp.maximum(got_ref[:SLABS, 16, :] + got_ref[SLABS:, 16, :], 1.0)
    got_ref[:SLABS, :16, :] = got_ref[:SLABS, :16, :] + got_ref[SLABS:, :16, :]
    amplitude = []
    for pm in range(2):
        columns = []
        for zh in range(2):
            planes = []
            for x in range(PLANES):
                q = (pm * PLANES + x) * 2 + zh
                planes.append(jnp.sqrt(got_ref[:SLABS, q, :] * scale[:, q : q + 1]))
            columns.append(jnp.concatenate(planes, axis=0))
        amplitude.append(jnp.concatenate(columns, axis=1))
    flip_z = permutation(N, lambda row, column: ((row + column) & (N - 1)) == 0)

    def frequency(index):
        return PLANES * (index & (SLABS - 1)) + (index >> 6)

    flip_x = permutation(N, lambda row, column: ((frequency(row) + frequency(column)) & (N - 1)) == 0)
    mirrored = []
    for pm in range(2):
        high, low = halves(amplitude[pm])
        high = dot(flip_x, high).astype(jnp.bfloat16)
        low = dot(flip_x, low).astype(jnp.bfloat16)
        mirrored.append(dot(high, flip_z) + dot(low, flip_z))
    even = []
    for pm in range(2):
        partner = jnp.where(first == 1, mirrored[pm], mirrored[1 - pm])
        even.append(0.5 * (amplitude[pm] + partner))
    amplitude = jnp.concatenate([part[:, :HALF] for part in even], axis=1)
    return (
        jnp.where(packed_lanes(), amplitude, 2.0 * amplitude),
        jnp.concatenate([part[:, HALF:] for part in even], axis=1),
    )


def packed_lanes():
    return (lax.broadcasted_iota(jnp.int32, (N, N), 1) & (HALF - 1)) == 0


def tile(values, row, column):
    return values[row * 128 : (row + 1) * 128, column * 128 : (column + 1) * 128]


def send_forward(field, table_ref, rows_ref):
    partly = along_lanes(field, table_ref, 2)
    parts = []
    for c in range(2):
        parts.append(jnp.concatenate([partly[x * N : (x + 1) * N, c * HALF : (c + 1) * HALF] for x in range(2)], axis=1))
    result = turn(table_ref, parts[0], parts[1], -1)
    for x in range(2):
        for pm in range(2):
            for c in range(2):
                rows_ref[:, x * 4 + pm * 2 + c, :] = tile(result, pm, c * 2 + x)


def image_from(rows_ref, table_ref, length):
    planes = rows_ref.shape[1] // 4
    parts = []
    for c in range(2):
        columns = []
        for x in range(planes):
            columns.append(jnp.concatenate([rows_ref[:, x * 4 + pm * 2 + c, :] for pm in range(2)], axis=0))
        parts.append(jnp.concatenate(columns, axis=1))
    partly = turn(table_ref, parts[0], parts[1], 1, length)
    rows = []
    for x in range(planes):
        real = partly[:, x * HALF : (x + 1) * HALF]
        imag = partly[:, (planes + x) * HALF : (planes + x + 1) * HALF]
        rows.append(jnp.concatenate([real, imag], axis=1))
    return along_lanes(jnp.concatenate(rows, axis=0), table_ref, 2, True)


def updated(rows_ref, support_ref, density_ref, table_ref):
    image = image_from(rows_ref, table_ref, N)
    support = support_ref[...].reshape(2 * N, N)
    density = density_ref[...].reshape(2 * N, N)
    return jnp.where(support == 1, image, density - BETA * image)


def first_kernel(density_ref, table_ref, out_ref, rows_ref):
    send_forward(density_ref[...].reshape(2 * N, N), table_ref, rows_ref)
    out_ref[...] = coded(rows_ref[...])


def middle_kernel(got_ref, support_ref, density_ref, table_ref, out_ref, rows_ref, code_ref, sem):
    rows_ref[...] = decoded(got_ref[...])
    field = updated(rows_ref, support_ref, density_ref, table_ref)
    send_forward(field, table_ref, rows_ref)
    for copy in send_out(rows_ref, code_ref, out_ref, sem):
        copy.wait()


def keep_kernel(group_ref, got_ref, support_ref, density_ref, table_ref, own_ref, code_ref, rows_ref, field_ref):
    group = group_ref[0]
    rows_ref[...] = decoded(got_ref[...])
    field_ref[...] = updated(rows_ref, support_ref, density_ref, table_ref).reshape(2, N, N)
    own_ref[...] = field_ref[:, pl.ds(pl.multiple_of(group * HALF, HALF), HALF), :]
    code_ref[...] = coded(field_ref[:, pl.ds(pl.multiple_of((1 - group) * HALF, HALF), HALF), :])


def last_kernel(group_ref, got_ref, support_ref, own_ref, other_ref, table_ref, field_ref, rows_ref):
    group = group_ref[0]
    rows_ref[...] = decoded(got_ref[...])
    image = image_from(rows_ref, table_ref, HALF).reshape(PLANES, HALF, N)
    other = decoded(other_ref[...])
    own = own_ref[...]
    for p in range(2):
        before = jnp.where(group == p, own, other)
        part = image[2 * p : 2 * p + 2]
        inside = support_ref[2 * p : 2 * p + 2] == 1
        field_ref[2 * p : 2 * p + 2] = jnp.where(inside, part, before - BETA * part)


PACKET = jax.ShapeDtypeStruct((DEVS, 8, 128), jnp.int16)
WIDE_PACKET = jax.ShapeDtypeStruct((DEVS, 16, 128), jnp.int16)


def scratch(rows):
    return pltpu.VMEM((DEVS, rows, 128), jnp.float32)


def first_field(density, t):
    return call(
        first_kernel, PACKET, in_specs=spec_vmem(2), out_specs=spec_vmem(1)[0], scratch_shapes=[scratch(8)]
    )(density, t["field"])


def middle_field(got, support, density, t):
    return call(
        middle_kernel,
        PACKET,
        in_specs=spec_vmem(4),
        out_specs=hbm(),
        scratch_shapes=[scratch(8), code_scratch(8), sems(BLOCKS)],
    )(got, support, density, t["field"])


def kept_field(group, got, support, density, t):
    shape = (2, HALF, N)
    return call(
        keep_kernel,
        (jax.ShapeDtypeStruct(shape, jnp.float32), jax.ShapeDtypeStruct(shape, jnp.int16)),
        in_specs=[smem()] + spec_vmem(4),
        out_specs=tuple(spec_vmem(2)),
        scratch_shapes=[scratch(8), pltpu.VMEM((2, N, N), jnp.float32)],
    )(group, got, support, density, t["field"])


def last_field(group, got, support, own, other, t):
    return call(
        last_kernel,
        jax.ShapeDtypeStruct((PLANES, HALF, N), jnp.float32),
        in_specs=[smem()] + spec_vmem(5),
        out_specs=spec_vmem(1)[0],
        scratch_shapes=[scratch(16)],
    )(group, got, support, own, other, t["field"])


def project(first, rows_ref, start, amplitude, nyquist, table_ref):
    lanes = []
    for c in range(2):
        for pm in range(2):
            parts = []
            for g in range(2):
                for x in range(2):
                    parts.append(rows_ref[g * SLABS : (g + 1) * SLABS, start + x * 4 + pm * 2 + c, :])
            lanes.append(jnp.concatenate(parts, axis=0))
    high, low = halves(jnp.concatenate(lanes, axis=1))
    right = jnp.concatenate([high, high, low], axis=0)
    by_cos = dot(jnp.concatenate(table_at(table_ref, 0), axis=1), right)
    by_sin = dot(jnp.concatenate(table_at(table_ref, 1), axis=1), right)
    real = by_cos[:, :N] + by_sin[:, N:]
    imag = by_cos[:, N:] - by_sin[:, :N]
    mirror_real = by_cos[:, :N] - by_sin[:, N:]
    mirror_imag = by_cos[:, N:] + by_sin[:, :N]

    def partner(mirror):
        return jnp.where(first == 1, mirror, jnp.concatenate([mirror[:, HALF:], mirror[:, :HALF]], axis=1))

    mirror_real = partner(mirror_real)
    mirror_imag = partner(mirror_imag)
    scale = amplitude * lax.rsqrt(real * real + imag * imag + SOFTEN)
    zero_real = 0.5 * (real + mirror_real)
    zero_imag = 0.5 * (imag - mirror_imag)
    top_real = 0.5 * (imag + mirror_imag)
    top_imag = 0.5 * (mirror_real - real)
    zero_scale = amplitude * lax.rsqrt(zero_real * zero_real + zero_imag * zero_imag + SOFTEN)
    top_scale = nyquist * lax.rsqrt(top_real * top_real + top_imag * top_imag + SOFTEN)
    packed = packed_lanes()
    new_real = jnp.where(packed, zero_scale * zero_real - top_scale * top_imag, scale * real)
    new_imag = jnp.where(packed, zero_scale * zero_imag + top_scale * top_real, scale * imag)
    return turn(table_ref, new_real, new_imag, 1)


def part_of(result, x, pm, c):
    lane = (c * 2 + pm) * HALF
    return result[x * SLABS : (x + 1) * SLABS, lane : lane + HALF]


def once_kernel(place_ref, got_ref, table_ref, out_ref, rows_ref, code_ref, sem):
    first = place_ref[0]
    rows_ref[...] = decoded(got_ref[...])
    amplitude, nyquist = amplitudes(first, rows_ref)
    result = project(first, rows_ref, 24, amplitude, nyquist, table_ref)
    for pm in range(2):
        for c in range(2):
            for g in range(2):
                for x in range(2):
                    rows_ref[g * SLABS : (g + 1) * SLABS, x * 4 + pm * 2 + c, :] = part_of(result, g * 2 + x, pm, c)
    for copy in send_out(rows_ref, code_ref, out_ref, sem):
        copy.wait()


def even_kernel(place_ref, got_ref, even_ref, rows_ref):
    rows_ref[...] = decoded(got_ref[:, :24, :])
    amplitude, nyquist = amplitudes(place_ref[0], rows_ref)
    even_ref[:N] = amplitude
    even_ref[N:] = nyquist


def again_kernel(
    place_ref, got_ref, even_ref, table_ref, out_hbm, rows_ref, code_ref, sem
):
    sign = place_ref[1]
    rows_ref[:, :8, :] = decoded(got_ref[...])
    result = project(place_ref[0], rows_ref, 0, even_ref[:N], even_ref[N:], table_ref)
    for pm in range(2):
        for c in range(2):
            for x in range(PLANES):
                rows_ref[:SLABS, x * 4 + pm * 2 + c, :] = part_of(result, x, pm, c)
    sent = []
    for block in range(2):
        slabs = pl.ds(block * 32, 32)
        others = pl.ds(SLABS + block * 32, 32)
        codes = coded(rows_ref[slabs]).astype(jnp.int32)
        code_ref[slabs] = codes.astype(jnp.int16)
        code_ref[others] = (sign * codes).astype(jnp.int16)
        sent.append(fetch(code_ref.at[slabs], out_hbm.at[slabs], sem.at[2 * block]))
        sent.append(fetch(code_ref.at[others], out_hbm.at[others], sem.at[2 * block + 1]))
    for copy in sent:
        copy.wait()


EVEN = jax.ShapeDtypeStruct((2 * N, N), jnp.float32)


def project_once(place, got, t):
    return call(
        once_kernel,
        PACKET,
        in_specs=[smem()] + spec_vmem(2),
        out_specs=hbm(),
        scratch_shapes=[scratch(32), code_scratch(8), sems(BLOCKS)],
    )(place, got, t["slab"])


def kept_amplitude(place, got):
    return call(
        even_kernel, EVEN, in_specs=[smem()] + spec_vmem(1), out_specs=spec_vmem(1)[0], scratch_shapes=[scratch(24)]
    )(place, got)


def project_again(place, got, even, t):
    return call(
        again_kernel,
        WIDE_PACKET,
        in_specs=[smem()] + spec_vmem(3),
        out_specs=hbm(),
        scratch_shapes=[scratch(16), code_scratch(16), sems(BLOCKS)],
    )(place, got, even, t["slab"])


def exchange(packet):
    return lax.all_to_all(packet, BOTH, split_axis=0, concat_axis=0, tiled=True)


def swap(array):
    return lax.ppermute(array, "grp", [(0, 1), (1, 0)])


def local(patterns, probabilities, source_row, target_row, support, density):
    t = tables()
    group = lax.axis_index("grp")
    slab = lax.axis_index("slab")
    device = group * SLABS + slab
    place = jnp.stack([(device == 0).astype(jnp.int32), 1 - 2 * (device & 1)])
    pad = ((0, 0), (0, 128 - CAP))
    target = target_row[0, 0]

    def planes_of(first):
        return [lax.dynamic_slice_in_dim(field, first, 2, 0) for field in (density, support)]

    theirs = jnp.stack([field.astype(jnp.float16) for field in planes_of(2 * (1 - group))])
    other = swap(theirs)
    send = gather_rows(source_row[0, 0], jnp.swapaxes(probabilities, 1, 2), patterns[0])
    send, other = lax.optimization_barrier((send, other))
    got = lax.all_to_all(send, "slab", split_axis=0, concat_axis=0, tiled=True)

    def whole(own, other):
        other = other.astype(own.dtype)
        return jnp.concatenate([jnp.where(group == 0, own, other), jnp.where(group == 0, other, own)], axis=1)

    planes, inside = [whole(own, other[i]) for i, own in enumerate(planes_of(2 * group))]
    packet = first_field(planes, t)
    sums = place_rows(got, target.reshape(SLABS // SOURCES, 1, TAKEN), jnp.pad(target, pad), packet)
    got_sums = exchange(sums)

    theirs = lax.dynamic_slice_in_dim(sums, (1 - group) * 8, 8, 1)
    other = swap(jnp.concatenate([theirs, sums[:, 16:24]], axis=1))
    intensity = intensity_of(group.reshape(1), sums, other)

    back = exchange(project_once(place, got_sums, t))
    back, even = lax.optimization_barrier((back, kept_amplitude(place, got_sums)))
    got = exchange(middle_field(back, inside, planes, t))
    own, theirs = kept_field(group.reshape(1), back, inside, planes, t)
    back = exchange(project_again(place, got, even, t))
    return (intensity, last_field(group.reshape(1), back, support, own, swap(theirs), t))


def solution(mesh):
    return jax.shard_map(
        local,
        mesh=mesh,
        in_specs=(
            P("grp", "slab", None),
            P("grp", "slab", None),
            P("grp", "slab", None, None),
            P("grp", "slab", None, None),
            P("slab", "grp", None),
            P("slab", "grp", None),
        ),
        out_specs=(P("slab", "grp", None), P("slab", "grp", None)),
        check_vma=False,
    )
```

```python
import functools

import jax
import jax.numpy as jnp
import ml_dtypes
import numpy as np
from jax import lax
from jax.experimental import pallas as pl
from jax.experimental.pallas import tpu as pltpu
from jax.sharding import PartitionSpec as P

N = 256
HALF = N // 2
PLANES = 4
SLABS = 64
DEVS = 128
CAP = 80
ROWS = 4096
BETA = 0.9
SOFTEN = 0.25
BOTH = ("grp", "slab")
MIB = 1024 * 1024


def split_table(table):
    high = table.astype(np.float32).astype(ml_dtypes.bfloat16)
    low = (table - high.astype(np.float64)).astype(np.float32).astype(ml_dtypes.bfloat16)
    return (jnp.asarray(high), jnp.asarray(low))


def phase(rows, columns):
    angle = 2.0 * np.pi / N * ((rows[:, None] * columns[None, :]) % N)
    return (np.cos(angle) / np.sqrt(N), np.sin(angle) / np.sqrt(N))


@functools.cache
def tables():
    z = np.arange(N)
    cos, sin = phase(z, np.arange(HALF))
    nyquist = np.cos(np.pi * z) / np.sqrt(N)
    forward_z = np.concatenate([cos, -sin], axis=1)
    forward_z[:, HALF] = nyquist
    first = np.arange(DEVS)
    frequency = np.concatenate([first, np.where(first == 0, HALF, N - first)])
    cos_y, sin_y = phase(frequency, z)
    order = (np.arange(PLANES)[:, None] + PLANES * np.arange(SLABS)[None, :]).reshape(-1)
    cos_x, sin_x = phase(order, order)

    def split(parts):
        rows = []
        for part in parts:
            high = part.astype(np.float32).astype(ml_dtypes.bfloat16)
            rows += [high, (part - high.astype(np.float64)).astype(np.float32).astype(ml_dtypes.bfloat16)]
        return jnp.asarray(np.concatenate(rows, axis=0))

    return dict(field=split([cos_y, sin_y, forward_z]), slab=split([cos_x, sin_x]))


def halves(values):
    high = values.astype(jnp.bfloat16)
    return (high, (values - high.astype(jnp.float32)).astype(jnp.bfloat16))


def dot(left, right):
    return jnp.dot(left, right, preferred_element_type=jnp.float32)


def table_at(ref, index):
    high = ref[2 * index * N : (2 * index + 1) * N]
    low = ref[(2 * index + 1) * N : (2 * index + 2) * N]
    return [high, low, high]


def along_lanes(values, ref, index, back=False):
    high, low = halves(values)
    top, rest, unused = table_at(ref, index)
    left = jnp.concatenate([high, low, high], axis=1)
    if back:
        right = jnp.concatenate([top, top, rest], axis=1)
        return lax.dot_general(left, right, (((1,), (1,)), ((), ())), preferred_element_type=jnp.float32)
    return dot(left, jnp.concatenate([top, top, rest], axis=0))


def turn(ref, real, imag, sign, back=None):
    real = halves(real)
    imag = halves(imag)
    straight = [jnp.concatenate([a, b], axis=1) for a, b in zip(real, imag)]
    if sign > 0:
        crossed = [jnp.concatenate([-b, a], axis=1) for a, b in zip(real, imag)]
    else:
        crossed = [jnp.concatenate([b, -a], axis=1) for a, b in zip(real, imag)]
    left = table_at(ref, 0) + table_at(ref, 1)
    right = [straight[0], straight[0], straight[1], crossed[0], crossed[0], crossed[1]]
    right = jnp.concatenate(right, axis=0)
    if back is None:
        return dot(jnp.concatenate(left, axis=1), right)
    left = jnp.concatenate(left, axis=0)[:, :back]
    return lax.dot_general(left, right, (((0,), (0,)), ((), ())), preferred_element_type=jnp.float32)


def permutation(size, matches):
    row = lax.broadcasted_iota(jnp.int32, (size, size), 0)
    column = lax.broadcasted_iota(jnp.int32, (size, size), 1)
    return matches(row, column).astype(jnp.bfloat16)


FINE = 2.0**14
OCTAVE = 32767.0 / 30.0
LOG2 = float(np.log(2.0))


def coded(values):
    size = jnp.minimum(jnp.log(1.0 + FINE * jnp.abs(values)) * (OCTAVE / LOG2), 32767.0)
    whole = (size + 0.5).astype(jnp.int32)
    return jnp.where(values < 0.0, -whole, whole).astype(jnp.int16)


def decoded(codes):
    values = codes.astype(jnp.int32).astype(jnp.float32)
    size = (jnp.exp(jnp.abs(values) * (LOG2 / OCTAVE)) - 1.0) * (1.0 / FINE)
    return jnp.where(values < 0.0, -size, size)


def call(kernel, out_shape, mib=16, **kwargs):
    return pl.pallas_call(
        kernel,
        out_shape=out_shape,
        compiler_params=pltpu.CompilerParams(vmem_limit_bytes=mib * MIB),
        **kwargs,
    )


def spec_vmem(count):
    return [pl.BlockSpec(memory_space=pltpu.VMEM)] * count


def smem():
    return pl.BlockSpec(memory_space=pltpu.SMEM)


def hbm():
    return pl.BlockSpec(memory_space=pltpu.HBM)


def fetch(source, target, sem):
    copy = pltpu.make_async_copy(source, target, sem)
    copy.start()
    return copy


BLOCKS = 4


def send_out(rows_ref, code_ref, out_ref, sems):
    count = code_ref.shape[1]
    copies = []
    for block in range(BLOCKS):
        devices = pl.ds(block * (DEVS // BLOCKS), DEVS // BLOCKS)
        code_ref[devices] = coded(rows_ref[devices, :count, :])
        copies.append(fetch(code_ref.at[devices], out_ref.at[devices], sems.at[block]))
    return copies


def code_scratch(rows):
    return pltpu.VMEM((DEVS, rows, 128), jnp.int16)


def sems(count):
    return pltpu.SemaphoreType.DMA((count,))


CUTS = 8
CUT = DEVS // CUTS
EMPTY = 8
SEND = 88


def gather_kernel(
    index_ref, table_ref, probabilities_ref, patterns_ref, out_hbm, block_ref, rows_ref, picked_ref, out_ref, sem
):
    def copy(cut):
        part = pl.ds(cut * CUT * 128, CUT * 128)
        return pltpu.make_async_copy(patterns_ref.at[:, part], block_ref.at[:, part], sem.at[cut])

    for cut in range(CUTS):
        copy(cut).start()
    rows_ref[:EMPTY] = jnp.zeros((EMPTY, 128), jnp.float32)
    left = probabilities_ref[0]
    weight = jnp.sum(left.astype(jnp.float32), axis=1, keepdims=True).astype(jnp.bfloat16).astype(jnp.float32)
    orientation = table_ref[...] >> 7
    weights = jnp.zeros((SLABS, CAP), jnp.float32)
    for r in range(32):
        weights = jnp.where(orientation == r, weight[r : r + 1], weights)
    weights = jnp.concatenate([weights, jnp.zeros((SLABS, 128 - CAP), jnp.float32)], axis=1)
    out_ref[:, CAP:, :] = jnp.broadcast_to(weights[:, None, :], (SLABS, 8, 128)).astype(jnp.bfloat16)
    for cut in range(CUTS):
        copy(cut).wait()
        part = dot(left, block_ref[:, cut * CUT * 128 : (cut + 1) * CUT * 128])
        part = part.astype(jnp.bfloat16).astype(jnp.float32)
        for d in range(CUT):
            rows_ref[pl.ds(EMPTY + cut * CUT + d, 32, stride=128), :] = part[:, d * 128 : (d + 1) * 128]

    sent = []
    for part in range(BLOCKS):
        owners = SLABS // BLOCKS
        for o in range(part * owners, (part + 1) * owners):
            for c in range(CAP):
                picked_ref[o * CAP + c : o * CAP + c + 1, :] = rows_ref[pl.ds(EMPTY + index_ref[o, c], 1), :]
        picked = picked_ref[part * owners * CAP : (part + 1) * owners * CAP].astype(jnp.bfloat16)
        block = pl.ds(part * owners, owners)
        out_ref[block, :CAP, :] = picked.reshape(owners, CAP, 128)
        sent.append(fetch(out_ref.at[block], out_hbm.at[block], sem.at[part]))
    for copy in sent:
        copy.wait()


def gather_rows(source, probabilities, patterns):
    return call(
        gather_kernel,
        jax.ShapeDtypeStruct((SLABS, SEND, 128), jnp.bfloat16),
        mib=60,
        cost_estimate=pl.CostEstimate(flops=2 * 32 * 256 * 16384, bytes_accessed=32 * MIB, transcendentals=0),
        in_specs=[smem()] + spec_vmem(2) + [hbm()],
        out_specs=hbm(),
        scratch_shapes=[
            pltpu.VMEM((256, DEVS * 128), jnp.bfloat16),
            pltpu.VMEM((EMPTY + ROWS, 128), jnp.float32),
            pltpu.VMEM((SLABS * CAP, 128), jnp.float32),
            pltpu.VMEM((SLABS, SEND, 128), jnp.bfloat16),
            sems(CUTS),
        ],
    )(source, source, probabilities, patterns)


SOURCES = 16
TAKEN = SOURCES * CAP
SLOTS = SLABS * CAP


def moved(target):
    y = (target >> 1) & (N - 1)
    pm = y >> 7
    j = jnp.where(pm == 1, (N - y) & (HALF - 1), y)
    return j * 16 + pm * 8 + (target >> 9) * 2 + (target & 1)


def columns_of(table):
    count = table.shape[0]
    square = jnp.concatenate([table, jnp.zeros((128 - count, 128), table.dtype)], axis=0).T
    return jnp.concatenate([square[:CAP, s : s + 1] for s in range(count)], axis=0)


def place_kernel(got_ref, row_ref, column_ref, packet_ref, out_ref, sum_ref, code_ref, sem):
    steps = SLABS // SOURCES
    code_ref[:, 24:, :] = packet_ref[...]
    last = got_ref[:, CAP:, :].astype(jnp.float32)[:, 0, :]
    total = jnp.zeros((32, 128), jnp.float32)
    lane = lax.broadcasted_iota(jnp.int32, (TAKEN, 128), 1).astype(jnp.float32).astype(jnp.bfloat16)
    zero = jnp.bfloat16(0)
    for step in range(steps):
        row = moved(row_ref[step])
        onehot = (lax.broadcasted_iota(jnp.int32, (512, TAKEN), 0) == (row & 511)).astype(jnp.bfloat16)
        rows = got_ref[step * SOURCES : (step + 1) * SOURCES, :CAP].reshape(TAKEN, 128)
        column = moved(column_ref[step * SOURCES : (step + 1) * SOURCES])
        mark = columns_of((((column >> 9) * 16) + (column & 15)).astype(jnp.float32))
        mark = jnp.broadcast_to(mark, (TAKEN, 128)).astype(jnp.bfloat16)
        above = [rows] + [jnp.where(mark >= jnp.bfloat16(16 * q), rows, zero) for q in range(1, 4)]
        parts = [jnp.where(mark < jnp.bfloat16(16 * q + 16), above[q], zero) for q in range(3)] + [above[3]]
        part = dot(onehot, jnp.concatenate(parts, axis=1))
        sum_ref[...] = part if step == 0 else sum_ref[...] + part
        weights = [last[step * SOURCES + s : step * SOURCES + s + 1, :CAP] for s in range(SOURCES)]
        weights = jnp.concatenate(weights, axis=1)
        device = lax.broadcasted_iota(jnp.int32, (32, TAKEN), 0) == ((row >> 4) & 31)
        left = jnp.where(device, weights, 0.0).astype(jnp.bfloat16)
        total += dot(left, jnp.where(mark == lane, jnp.bfloat16(1), zero))
    total = coded(total).astype(jnp.int32)
    sent = []
    for q in range(4):
        devices = pl.ds(q * 32, 32)
        part = sum_ref[:, q * 128 : (q + 1) * 128].reshape(32, 16, 128)
        code_ref[devices, :16, :] = coded(part)
        entries = total if q == 0 else jnp.concatenate([total[:, 16 * q :], total[:, : 16 * q]], axis=1)
        code_ref[devices, 16:24, :] = jnp.broadcast_to(entries[:, None, :], (32, 8, 128)).astype(jnp.int16)
        sent.append(fetch(code_ref.at[devices], out_ref.at[devices], sem.at[q]))
    for copy in sent:
        copy.wait()


def place_rows(got, row, column, packet):
    return call(
        place_kernel,
        jax.ShapeDtypeStruct((DEVS, 32, 128), jnp.int16),
        mib=28,
        in_specs=spec_vmem(4),
        out_specs=hbm(),
        scratch_shapes=[
            pltpu.VMEM((512, 512), jnp.float32),
            code_scratch(32),
            sems(4),
        ],
    )(got, row, column, packet)


def intensity_kernel(group_ref, own_ref, other_ref, out_ref):
    group = group_ref[0]
    own = decoded(own_ref[:, :24, :])
    other = decoded(other_ref[...])
    total = jnp.where(group == 0, own[:, :8, :], own[:, 8:16, :]) + other[:, :8, :]
    weights = own[:, 16, :] + other[:, 8, :]
    divisor = jnp.maximum(jnp.where(group == 0, weights[:, :8], weights[:, 8:16]), 1.0)
    wide = jnp.concatenate([total[:, q, :] / divisor[:, q : q + 1] for q in range(8)], axis=1)
    same = permutation(HALF, lambda row, column: row == column)
    mirrored = permutation(HALF, lambda row, column: ((row + column) & (HALF - 1)) == 0)
    flip = jnp.where(group == 0, same, mirrored)
    high, low = halves(wide)
    turned = dot(flip, high) + dot(flip, low)
    for x in range(PLANES):
        out_ref[x] = turned[:, x * N : (x + 1) * N]


def intensity_of(group, own, other):
    return call(
        intensity_kernel,
        jax.ShapeDtypeStruct((PLANES, HALF, N), jnp.float32),
        in_specs=[smem()] + spec_vmem(2),
        out_specs=spec_vmem(1)[0],
    )(group, own, other)


def amplitudes(first, got_ref):
    scale = 1.0 / jnp.maximum(got_ref[:SLABS, 16, :] + got_ref[SLABS:, 16, :], 1.0)
    got_ref[:SLABS, :16, :] = got_ref[:SLABS, :16, :] + got_ref[SLABS:, :16, :]
    amplitude = []
    for pm in range(2):
        columns = []
        for zh in range(2):
            planes = []
            for x in range(PLANES):
                q = (pm * PLANES + x) * 2 + zh
                planes.append(jnp.sqrt(got_ref[:SLABS, q, :] * scale[:, q : q + 1]))
            columns.append(jnp.concatenate(planes, axis=0))
        amplitude.append(jnp.concatenate(columns, axis=1))
    flip_z = permutation(N, lambda row, column: ((row + column) & (N - 1)) == 0)

    def frequency(index):
        return PLANES * (index & (SLABS - 1)) + (index >> 6)

    flip_x = permutation(N, lambda row, column: ((frequency(row) + frequency(column)) & (N - 1)) == 0)
    mirrored = []
    for pm in range(2):
        high, low = halves(amplitude[pm])
        high = dot(flip_x, high).astype(jnp.bfloat16)
        low = dot(flip_x, low).astype(jnp.bfloat16)
        mirrored.append(dot(high, flip_z) + dot(low, flip_z))
    even = []
    for pm in range(2):
        partner = jnp.where(first == 1, mirrored[pm], mirrored[1 - pm])
        even.append(0.5 * (amplitude[pm] + partner))
    amplitude = jnp.concatenate([part[:, :HALF] for part in even], axis=1)
    return (
        jnp.where(packed_lanes(), amplitude, 2.0 * amplitude),
        jnp.concatenate([part[:, HALF:] for part in even], axis=1),
    )


def packed_lanes():
    return (lax.broadcasted_iota(jnp.int32, (N, N), 1) & (HALF - 1)) == 0


def tile(values, row, column):
    return values[row * 128 : (row + 1) * 128, column * 128 : (column + 1) * 128]


def send_forward(field, table_ref, rows_ref):
    partly = along_lanes(field, table_ref, 2)
    parts = []
    for c in range(2):
        parts.append(jnp.concatenate([partly[x * N : (x + 1) * N, c * HALF : (c + 1) * HALF] for x in range(2)], axis=1))
    result = turn(table_ref, parts[0], parts[1], -1)
    for x in range(2):
        for pm in range(2):
            for c in range(2):
                rows_ref[:, x * 4 + pm * 2 + c, :] = tile(result, pm, c * 2 + x)


def image_from(rows_ref, table_ref, length):
    planes = rows_ref.shape[1] // 4
    parts = []
    for c in range(2):
        columns = []
        for x in range(planes):
            columns.append(jnp.concatenate([rows_ref[:, x * 4 + pm * 2 + c, :] for pm in range(2)], axis=0))
        parts.append(jnp.concatenate(columns, axis=1))
    partly = turn(table_ref, parts[0], parts[1], 1, length)
    rows = []
    for x in range(planes):
        real = partly[:, x * HALF : (x + 1) * HALF]
        imag = partly[:, (planes + x) * HALF : (planes + x + 1) * HALF]
        rows.append(jnp.concatenate([real, imag], axis=1))
    return along_lanes(jnp.concatenate(rows, axis=0), table_ref, 2, True)


def updated(rows_ref, support_ref, density_ref, table_ref):
    image = image_from(rows_ref, table_ref, N)
    support = support_ref[...].reshape(2 * N, N)
    density = density_ref[...].reshape(2 * N, N)
    return jnp.where(support == 1, image, density - BETA * image)


def first_kernel(density_ref, table_ref, out_ref, rows_ref):
    send_forward(density_ref[...].reshape(2 * N, N), table_ref, rows_ref)
    out_ref[...] = coded(rows_ref[...])


def middle_kernel(got_ref, support_ref, density_ref, table_ref, out_ref, rows_ref, code_ref, sem):
    rows_ref[...] = decoded(got_ref[...])
    field = updated(rows_ref, support_ref, density_ref, table_ref)
    send_forward(field, table_ref, rows_ref)
    for copy in send_out(rows_ref, code_ref, out_ref, sem):
        copy.wait()


def keep_kernel(group_ref, got_ref, support_ref, density_ref, table_ref, own_ref, code_ref, rows_ref, field_ref):
    group = group_ref[0]
    rows_ref[...] = decoded(got_ref[...])
    field_ref[...] = updated(rows_ref, support_ref, density_ref, table_ref).reshape(2, N, N)
    own_ref[...] = field_ref[:, pl.ds(pl.multiple_of(group * HALF, HALF), HALF), :]
    code_ref[...] = coded(field_ref[:, pl.ds(pl.multiple_of((1 - group) * HALF, HALF), HALF), :])


def last_kernel(group_ref, got_ref, support_ref, own_ref, other_ref, table_ref, field_ref, rows_ref):
    group = group_ref[0]
    rows_ref[...] = decoded(got_ref[...])
    image = image_from(rows_ref, table_ref, HALF).reshape(PLANES, HALF, N)
    other = decoded(other_ref[...])
    own = own_ref[...]
    for p in range(2):
        before = jnp.where(group == p, own, other)
        part = image[2 * p : 2 * p + 2]
        inside = support_ref[2 * p : 2 * p + 2] == 1
        field_ref[2 * p : 2 * p + 2] = jnp.where(inside, part, before - BETA * part)


PACKET = jax.ShapeDtypeStruct((DEVS, 8, 128), jnp.int16)
WIDE_PACKET = jax.ShapeDtypeStruct((DEVS, 16, 128), jnp.int16)


def scratch(rows):
    return pltpu.VMEM((DEVS, rows, 128), jnp.float32)


def first_field(density, t):
    return call(
        first_kernel, PACKET, in_specs=spec_vmem(2), out_specs=spec_vmem(1)[0], scratch_shapes=[scratch(8)]
    )(density, t["field"])


def middle_field(got, support, density, t):
    return call(
        middle_kernel,
        PACKET,
        in_specs=spec_vmem(4),
        out_specs=hbm(),
        scratch_shapes=[scratch(8), code_scratch(8), sems(BLOCKS)],
    )(got, support, density, t["field"])


def kept_field(group, got, support, density, t):
    shape = (2, HALF, N)
    return call(
        keep_kernel,
        (jax.ShapeDtypeStruct(shape, jnp.float32), jax.ShapeDtypeStruct(shape, jnp.int16)),
        in_specs=[smem()] + spec_vmem(4),
        out_specs=tuple(spec_vmem(2)),
        scratch_shapes=[scratch(8), pltpu.VMEM((2, N, N), jnp.float32)],
    )(group, got, support, density, t["field"])


def last_field(group, got, support, own, other, t):
    return call(
        last_kernel,
        jax.ShapeDtypeStruct((PLANES, HALF, N), jnp.float32),
        in_specs=[smem()] + spec_vmem(5),
        out_specs=spec_vmem(1)[0],
        scratch_shapes=[scratch(16)],
    )(group, got, support, own, other, t["field"])


def project(first, rows_ref, start, amplitude, nyquist, table_ref):
    lanes = []
    for c in range(2):
        for pm in range(2):
            parts = []
            for g in range(2):
                for x in range(2):
                    parts.append(rows_ref[g * SLABS : (g + 1) * SLABS, start + x * 4 + pm * 2 + c, :])
            lanes.append(jnp.concatenate(parts, axis=0))
    high, low = halves(jnp.concatenate(lanes, axis=1))
    right = jnp.concatenate([high, high, low], axis=0)
    by_cos = dot(jnp.concatenate(table_at(table_ref, 0), axis=1), right)
    by_sin = dot(jnp.concatenate(table_at(table_ref, 1), axis=1), right)
    real = by_cos[:, :N] + by_sin[:, N:]
    imag = by_cos[:, N:] - by_sin[:, :N]
    mirror_real = by_cos[:, :N] - by_sin[:, N:]
    mirror_imag = by_cos[:, N:] + by_sin[:, :N]

    def partner(mirror):
        return jnp.where(first == 1, mirror, jnp.concatenate([mirror[:, HALF:], mirror[:, :HALF]], axis=1))

    mirror_real = partner(mirror_real)
    mirror_imag = partner(mirror_imag)
    scale = amplitude * lax.rsqrt(real * real + imag * imag + SOFTEN)
    zero_real = 0.5 * (real + mirror_real)
    zero_imag = 0.5 * (imag - mirror_imag)
    top_real = 0.5 * (imag + mirror_imag)
    top_imag = 0.5 * (mirror_real - real)
    zero_scale = amplitude * lax.rsqrt(zero_real * zero_real + zero_imag * zero_imag + SOFTEN)
    top_scale = nyquist * lax.rsqrt(top_real * top_real + top_imag * top_imag + SOFTEN)
    packed = packed_lanes()
    new_real = jnp.where(packed, zero_scale * zero_real - top_scale * top_imag, scale * real)
    new_imag = jnp.where(packed, zero_scale * zero_imag + top_scale * top_real, scale * imag)
    return turn(table_ref, new_real, new_imag, 1)


def part_of(result, x, pm, c):
    lane = (c * 2 + pm) * HALF
    return result[x * SLABS : (x + 1) * SLABS, lane : lane + HALF]


def once_kernel(place_ref, got_ref, table_ref, out_ref, rows_ref, code_ref, sem):
    first = place_ref[0]
    rows_ref[...] = decoded(got_ref[...])
    amplitude, nyquist = amplitudes(first, rows_ref)
    result = project(first, rows_ref, 24, amplitude, nyquist, table_ref)
    for pm in range(2):
        for c in range(2):
            for g in range(2):
                for x in range(2):
                    rows_ref[g * SLABS : (g + 1) * SLABS, x * 4 + pm * 2 + c, :] = part_of(result, g * 2 + x, pm, c)
    for copy in send_out(rows_ref, code_ref, out_ref, sem):
        copy.wait()


def even_kernel(place_ref, got_ref, even_ref, rows_ref):
    rows_ref[...] = decoded(got_ref[:, :24, :])
    amplitude, nyquist = amplitudes(place_ref[0], rows_ref)
    even_ref[:N] = amplitude
    even_ref[N:] = nyquist


def again_kernel(
    place_ref, got_ref, even_ref, table_ref, out_hbm, rows_ref, code_ref, sem
):
    sign = place_ref[1]
    rows_ref[:, :8, :] = decoded(got_ref[...])
    result = project(place_ref[0], rows_ref, 0, even_ref[:N], even_ref[N:], table_ref)
    for pm in range(2):
        for c in range(2):
            for x in range(PLANES):
                rows_ref[:SLABS, x * 4 + pm * 2 + c, :] = part_of(result, x, pm, c)
    sent = []
    for block in range(2):
        slabs = pl.ds(block * 32, 32)
        others = pl.ds(SLABS + block * 32, 32)
        codes = coded(rows_ref[slabs]).astype(jnp.int32)
        code_ref[slabs] = codes.astype(jnp.int16)
        code_ref[others] = (sign * codes).astype(jnp.int16)
        sent.append(fetch(code_ref.at[slabs], out_hbm.at[slabs], sem.at[2 * block]))
        sent.append(fetch(code_ref.at[others], out_hbm.at[others], sem.at[2 * block + 1]))
    for copy in sent:
        copy.wait()


EVEN = jax.ShapeDtypeStruct((2 * N, N), jnp.float32)


def project_once(place, got, t):
    return call(
        once_kernel,
        PACKET,
        in_specs=[smem()] + spec_vmem(2),
        out_specs=hbm(),
        scratch_shapes=[scratch(32), code_scratch(8), sems(BLOCKS)],
    )(place, got, t["slab"])


def kept_amplitude(place, got):
    return call(
        even_kernel, EVEN, in_specs=[smem()] + spec_vmem(1), out_specs=spec_vmem(1)[0], scratch_shapes=[scratch(24)]
    )(place, got)


def project_again(place, got, even, t):
    return call(
        again_kernel,
        WIDE_PACKET,
        in_specs=[smem()] + spec_vmem(3),
        out_specs=hbm(),
        scratch_shapes=[scratch(16), code_scratch(16), sems(BLOCKS)],
    )(place, got, even, t["slab"])


def exchange(packet):
    return lax.all_to_all(packet, BOTH, split_axis=0, concat_axis=0, tiled=True)


def swap(array):
    return lax.ppermute(array, "grp", [(0, 1), (1, 0)])


def local(patterns, probabilities, source_row, target_row, support, density):
    t = tables()
    group = lax.axis_index("grp")
    slab = lax.axis_index("slab")
    device = group * SLABS + slab
    place = jnp.stack([(device == 0).astype(jnp.int32), 1 - 2 * (device & 1)])
    pad = ((0, 0), (0, 128 - CAP))
    target = target_row[0, 0]

    def planes_of(first):
        return [lax.dynamic_slice_in_dim(field, first, 2, 0) for field in (density, support)]

    theirs = [field.astype(jnp.float16)[None] for field in planes_of(2 * (1 - group))]
    theirs = jnp.where(lax.broadcasted_iota(jnp.int32, (2, 1, 1, 1), 0) == 0, *theirs)
    other = swap(theirs)
    send = gather_rows(source_row[0, 0], jnp.swapaxes(probabilities, 1, 2), patterns[0])
    send, other = lax.optimization_barrier((send, other))
    got = lax.all_to_all(send, "slab", split_axis=0, concat_axis=0, tiled=True)

    def whole(own, other):
        other = other.astype(own.dtype)
        return jnp.concatenate([jnp.where(group == 0, own, other), jnp.where(group == 0, other, own)], axis=1)

    planes, inside = [whole(own, other[i]) for i, own in enumerate(planes_of(2 * group))]
    packet = first_field(planes, t)
    sums = place_rows(got, target.reshape(SLABS // SOURCES, 1, TAKEN), jnp.pad(target, pad), packet)
    got_sums = exchange(sums)

    theirs = lax.dynamic_slice_in_dim(sums, (1 - group) * 8, 8, 1)
    other = swap(jnp.concatenate([theirs, sums[:, 16:24]], axis=1))
    intensity = intensity_of(group.reshape(1), sums, other)

    back = exchange(project_once(place, got_sums, t))
    back, even = lax.optimization_barrier((back, kept_amplitude(place, got_sums)))
    got = exchange(middle_field(back, inside, planes, t))
    own, theirs = kept_field(group.reshape(1), back, inside, planes, t)
    back = exchange(project_again(place, got, even, t))
    return (intensity, last_field(group.reshape(1), back, support, own, swap(theirs), t))


def solution(mesh):
    return jax.shard_map(
        local,
        mesh=mesh,
        in_specs=(
            P("grp", "slab", None),
            P("grp", "slab", None),
            P("grp", "slab", None, None),
            P("grp", "slab", None, None),
            P("slab", "grp", None),
            P("slab", "grp", None),
        ),
        out_specs=(P("slab", "grp", None), P("slab", "grp", None)),
        check_vma=False,
    )
```
